128 devices in a mesh: dp: 8 (over z_hi, y), factor: 16 (over z_lo, x, core).
Axes of the slice: x: 4, y: 4, z: 4 (z_hi: 2, z_lo: 2; z = z_hi * 2 + z_lo), core: 2. Of those that a mesh axis runs over, the one named last changes fastest.
Arguments:
- features: bfloat16 [2048, 16, 2048], P('dp', 'factor'), may hold values from -135 to 135
- previous: float32 [16, 2048, 2048], P('factor'), may hold values from -40 to 40, as said below
- gradient: bfloat16 [16, 2, 2048, 2048], P('factor', None, 'dp'), may hold values from -6 to 6
Outputs:
- factor: float32 [16, 2048, 2048], P('factor', 'dp')
- preconditioned: bfloat16 [16, 2, 2048, 2048], P('factor', None, None, 'dp')
The draws below stay inside these ranges and needn't reach their ends.
Inputs may be any that keep to these rules, and one draw needn't show every extreme that they name: `previous`: every block is symmetric and positive definite.
All inputs are finite; a program needn't handle non-finite values.
Results may differ from the reference program's by a relative error of at most 0.0049.
Values may be sent and summed in bfloat16 or wider, within the bound.
A program may use at most 320 MiB of HBM per device.

```python
import math
import jax
import jax.numpy as jnp

BLK = 2048
TOKENS = 2048
LAYERS = 2
NBLK = 16


def block_scales():
    positions = jnp.arange(NBLK)
    member = positions // LAYERS
    rising = jnp.exp(math.log(3.0) * member.astype(jnp.float32) / 7.0)
    return rising * jnp.where(member % 2 == 1, 0.3, 1.0)


def draw_features(key, part):
    key = jax.random.fold_in(key, 11)
    subkeys = jax.random.split(key, 3)
    shape = (TOKENS, NBLK, BLK)
    col_scale = jnp.exp(jax.random.uniform(subkeys[1], (1, NBLK, BLK), minval=math.log(0.3), maxval=math.log(3.0)))
    token_scale = jnp.exp(jax.random.uniform(subkeys[0], (TOKENS, 1, 1), minval=math.log(0.3), maxval=math.log(3.0)))
    base_values = jax.random.truncated_normal(subkeys[2], -5.0, 5.0, shape)
    values = base_values * token_scale * col_scale * block_scales()[None, :, None]
    return values.astype(jnp.bfloat16)


def draw_previous(key, part):
    key = jax.random.fold_in(key, 23)
    subkeys = jax.random.split(key, 2)
    uniform_noise = jax.random.uniform(subkeys[0], (NBLK, BLK, BLK), minval=-1.0, maxval=1.0)
    symmetric = 0.5 * (uniform_noise + jnp.swapaxes(uniform_noise, 1, 2))
    row_scale = jnp.exp(jax.random.uniform(subkeys[1], (NBLK, BLK), minval=math.log(0.5), maxval=math.log(2.0)))
    row_scale = row_scale * block_scales()[:, None]
    unit_core = jnp.eye(BLK, dtype=jnp.float32)[None] + 0.5 / BLK * symmetric
    return (row_scale[:, :, None] * unit_core * row_scale[:, None, :]).astype(jnp.float32)


def shard_levels(own_key, shape, cuts, least, top_value):
    level = 1.0
    for axis_at, shards_of in cuts:
        draws = jax.random.uniform(jax.random.fold_in(jax.random.fold_in(own_key, 6), axis_at), (shards_of,), jnp.float32, least / len(cuts), top_value / len(cuts))
        level = level * jnp.repeat(jnp.exp(draws), shape[axis_at] // shards_of).reshape((-1,) + (1,) * (len(shape) - 1 - axis_at))
    return level


def gaussian(own_key, shape, scale, limit, cuts=(), kind=jnp.bfloat16):
    entries = scale * jax.random.normal(own_key, shape, jnp.float32)
    if cuts:
        entries = entries * shard_levels(own_key, shape, cuts, -0.22, 0.18)
    return jnp.clip(entries, -limit, limit).astype(kind)


def setup_inputs(seed: int = 0) -> dict:
    keys = jax.random.split(jax.random.key(seed), 4)
    return {
        "features": draw_features(jax.random.fold_in(keys[3], 71), 0),
        "previous": draw_previous(jax.random.fold_in(keys[3], 71), 0),
        "gradient": gaussian(keys[2], (NBLK, 2, BLK, BLK), 1.0, 6.0, ((0, 16), (2, 8))),
    }


decay_rate = 0.5
damping = 0.1

def solve_both(lower_factor, right_side):
    halfway = jax.scipy.linalg.solve_triangular(lower_factor, right_side, lower=True)
    return jax.scipy.linalg.solve_triangular(lower_factor, halfway, lower=True, trans=1)

def reference(features, previous, gradient):
    blocks = previous.shape[0]
    layers = blocks // 8
    weight = (1.0 - decay_rate) / TOKENS
    factors = []
    traces = []
    for block_index in range(blocks):
        column = features[:, block_index, :]
        gram_sum = jnp.dot(column.T.astype(jnp.float32), column.astype(jnp.float32), preferred_element_type=jnp.float32)
        factor = decay_rate * previous[block_index] + weight * gram_sum
        factors.append(factor)
        traces.append(jnp.trace(factor))
    lowers = []
    for block_index in range(blocks):
        layer_index = block_index % layers
        member = block_index // layers
        input_trace = traces[layer_index] + traces[layer_index + 2 * layers] + traces[layer_index + 4 * layers] + traces[layer_index + 6 * layers]
        grad_trace = traces[layer_index + layers] + traces[layer_index + 3 * layers] + traces[layer_index + 5 * layers] + traces[layer_index + 7 * layers]
        pi_ratio = jnp.sqrt(input_trace / grad_trace)
        if member % 2 == 0:
            diag_shift = pi_ratio * math.sqrt(damping)
        else:
            diag_shift = math.sqrt(damping) / pi_ratio
        size_eye = jnp.eye(factors[block_index].shape[0], dtype=jnp.float32)
        lowers.append(jnp.linalg.cholesky(factors[block_index] + diag_shift * size_eye))
    outputs = []
    for block_index in range(blocks):
        tile_list = []
        for tile_index in range(2):
            source = gradient[block_index, tile_index].astype(jnp.float32)
            section_one = solve_both(lowers[block_index], source.T).T.astype(jnp.bfloat16)
            partner = (block_index - layers * (2 * tile_index + 1)) % blocks
            finished = solve_both(lowers[partner], section_one.astype(jnp.float32))
            tile_list.append(finished.astype(jnp.bfloat16))
        outputs.append(jnp.stack(tile_list))
    return (jnp.stack(factors), jnp.stack(outputs))
```

```python
import math
import jax, jax.numpy as jnp, numpy as np, functools
from jax import lax
from jax.experimental import pallas as pl
from jax.experimental.pallas import tpu as pltpu
W=256

def inv2(a,b,c):
    r = 1.0/(a*c-b*b)
    return c*r, -b*r, a*r

def inv4(p):
    a,b,c = inv2(p[0][0],p[0][1],p[1][1])
    b00,b01,b10,b11 = p[0][2],p[0][3],p[1][2],p[1][3]
    w00=a*b00+b*b10; w01=a*b01+b*b11; w10=b*b00+c*b10; w11=b*b01+c*b11
    s00=p[2][2]-(b00*w00+b10*w10); s01=p[2][3]-(b00*w01+b10*w11); s11=p[3][3]-(b01*w01+b11*w11)
    d00,d01,d11=inv2(s00,s01,s11)
    x00=-(w00*d00+w01*d01); x01=-(w00*d01+w01*d11); x10=-(w10*d00+w11*d01); x11=-(w10*d01+w11*d11)
    t00=a-(x00*w00+x01*w01); t01=b-(x00*w10+x01*w11); t11=c-(x10*w10+x11*w11)
    return [[t00,t01,x00,x01],[t01,t11,x10,x11],[x00,x10,d00,d01],[x01,x11,d01,d11]]

def invq(p,q):
    if q==1: return [[1.0/p[0][0]]]
    if q==2:
        a,b,c=inv2(p[0][0],p[0][1],p[1][1]); return [[a,b],[b,c]]
    return inv4(p)

NN=(((1,),(0,)),((),())); NT=(((1,),(1,)),((),()))
bf=jnp.bfloat16; f32=jnp.float32
def split(x):
    hi=x.astype(bf); return hi,(x-hi.astype(f32)).astype(bf)
def dot3(a,b,dims):
    d=lambda x,y: lax.dot_general(x,y,dims,preferred_element_type=f32)
    return d(a[0],b[0])+(d(a[0],b[1])+d(a[1],b[0]))

def sweep(A, slot, q=4, n=128):
    lane = lax.broadcasted_iota(jnp.int32,(1,n),1)
    for s in range(0,n,q):
        rows=[A[s+i:s+i+1,:] for i in range(q)]
        p=[[jnp.broadcast_to(rows[i][:,s+j:s+j+1],(1,n)) if j>=i else None for j in range(q)] for i in range(q)]
        X=invq(p,q)
        inl=(lane>=s)&(lane<s+q)
        rm=[jnp.where(lane==s+i,1.0,jnp.where(inl,0.0,rows[i])) for i in range(q)]
        nr=[]
        for i in range(q):
            t=X[i][0]*rm[0]
            for j in range(1,q): t=t+X[i][j]*rm[j]
            nr.append(t)
        tiles=[]
        for r in range(0,n,8):
            T=A[r:r+8,:]
            cols=[jnp.broadcast_to(T[:,s+i:s+i+1],(8,n)) for i in range(q)]
            T=jnp.where(inl,0.0,T)
            if r<=s<r+8:
                ri=lax.broadcasted_iota(jnp.int32,(8,1),0)+r
                inr=(ri>=s)&(ri<s+q)
                T=jnp.where(inr,0.0,T)
                cols=[jnp.where(ri==s+i,-1.0,jnp.where(inr,0.0,cols[i])) for i in range(q)]
            for i in range(q): T=T-cols[i]*nr[i]
            tiles.append(T)
        A=jnp.concatenate(tiles,axis=0)
        slot(s//q)
    return A

def tables(nb, extra, slots):
    dst=np.zeros((nb,slots),np.int32); li=np.zeros((nb,slots),np.int32); rj=np.zeros((nb,slots),np.int32)
    dst[:]=nb-1
    for k in range(1,nb):
        t=0
        for j in range(k,nb):
            for i in range(j,nb+extra):
                if (i,j)==(k,k): continue
                dst[k,t]=i*nb+j; li[k,t]=i; rj[k,t]=j; t+=1
        assert t<=slots
    return dst,li,rj

def factor_kernel(nb, extra, interleave, dst_t, li_t, rj_t, a_hbm, g_hbm, chi_hbm, clo_hbm, phi_o, plo_o, s_o,
                  blk, chi, clo, uh, ul, ch, cl, half, asem, gsem, osem):
    nr=nb+extra
    copies=[]
    for j in range(nb):
        cs=[]
        for i in range(j,nb):
            cs.append(pltpu.make_async_copy(a_hbm.at[pl.ds(i*W,W),pl.ds(j*W,W)], blk.at[i*nb+j], asem.at[i,j]))
        for e in range(extra):
            cs.append(pltpu.make_async_copy(g_hbm.at[pl.ds(e*W,W),pl.ds(j*W,W)], blk.at[(nb+e)*nb+j], gsem.at[e,j]))
        for c in cs: c.start()
        copies+=cs
    for c in copies: c.wait()

    def tile(k,t):
        d=dst_t[k,t]; i=li_t[k,t]; j=rj_t[k,t]
        blk[d]=blk[d]-dot3((ch[i],cl[i]),(uh[j],ul[j]),NT)

    def step(k,_):
        kk=k*nb+k
        half[0]=blk[kk,:128,:128]
        def hbody(h,_):
            fn=(lambda s: tile(k,h*32+s)) if interleave else (lambda s:None)
            p=sweep(half[h],fn)
            half[h]=p
            @pl.when(h==0)
            def _():
                d21=split(blk[kk,128:,:128])
                w=dot3(d21,split(p),NN)
                half[2]=w
                half[1]=blk[kk,128:,128:]-dot3(split(w),d21,NT)
            return 0
        lax.fori_loop(0,2,hbody,0)
        p2=split(half[1]); w=half[2]
        x21=-dot3(p2,split(w),NN)
        wt=split(w.T)
        x11=half[0]-dot3(wt,split(x21),NN)
        x12=x21.T
        top=jnp.concatenate([x11,x12],axis=1)
        bot=jnp.concatenate([x21,half[1]],axis=1)
        P=split(jnp.concatenate([top,bot],axis=0))
        phi_o[k]=P[0]; plo_o[k]=P[1]
        if not interleave:
            def lp(t,_):
                tile(k,t); return 0
            lax.fori_loop(0,jnp.where(k==0,0,jnp.int32(64)),lp,0)
        def cbody(i,_):
            u=split(blk[i*nb+k])
            uh[i]=u[0]; ul[i]=u[1]
            c=dot3(u,(phi_o[k],plo_o[k]),NN)
            blk[i*nb+k]=c
            cs=split(c)
            ch[i]=cs[0]; cl[i]=cs[1]
            return 0
        lax.fori_loop(k+1,nr,cbody,0)
        def st(i,_):
            r=pl.ds(pl.multiple_of(i*W,W),W); c=pl.ds(pl.multiple_of(k*W,W),W)
            chi[r,c]=ch[i]; clo[r,c]=cl[i]
            return 0
        lax.fori_loop(k+1,nb,st,0)
        @pl.when(k+1<nb)
        def _():
            d=(k+1)*nb+k+1
            blk[d]=blk[d]-dot3((ch[k+1],cl[k+1]),(uh[k+1],ul[k+1]),NT)
        return 0
    lax.fori_loop(0,nb,step,0)
    o1=pltpu.make_async_copy(chi,chi_hbm,osem.at[0]); o2=pltpu.make_async_copy(clo,clo_hbm,osem.at[1])
    o1.start(); o2.start()
    for k in reversed(range(nb)):
        for e in range(extra):
            z=blk[(nb+e)*nb+k]
            for i in range(k+1,nb):
                cc=(chi[i*W:(i+1)*W,k*W:(k+1)*W],clo[i*W:(i+1)*W,k*W:(k+1)*W])
                xi=(blk_x(uh,ch,e,nb)[i], blk_x(ul,cl,e,nb)[i])
                z=z-dot3(xi,cc,NN)
            x=split(z)
            blk_x(uh,ch,e,nb)[k]=x[0]; blk_x(ul,cl,e,nb)[k]=x[1]
            s_o[e*W:(e+1)*W,k*W:(k+1)*W]=x[0]
    o1.wait(); o2.wait()
def blk_x(u,c,e,nb): return u if e==0 else c

def factor_call(a,g,interleave=True):
    n=a.shape[0]; nb=n//W; extra=g.shape[0]//W
    t=tables(nb,extra,64)
    sm=pl.BlockSpec(memory_space=pltpu.SMEM); an=pl.BlockSpec(memory_space=pl.ANY); vm=pl.BlockSpec(memory_space=pltpu.VMEM)
    return pl.pallas_call(
        functools.partial(factor_kernel,nb,extra,interleave),
        out_shape=(jax.ShapeDtypeStruct((n,n),bf),jax.ShapeDtypeStruct((n,n),bf),jax.ShapeDtypeStruct((nb,W,W),bf),jax.ShapeDtypeStruct((nb,W,W),bf),jax.ShapeDtypeStruct((extra*W,n),bf)),
        in_specs=[sm,sm,sm,an,an], out_specs=(an,an,vm,vm,vm),
        scratch_shapes=[pltpu.VMEM(((nb+extra)*nb,W,W),f32),pltpu.VMEM((n,n),bf),pltpu.VMEM((n,n),bf),
            pltpu.VMEM((nb+extra,W,W),bf),pltpu.VMEM((nb+extra,W,W),bf),pltpu.VMEM((nb+extra,W,W),bf),pltpu.VMEM((nb+extra,W,W),bf),
            pltpu.VMEM((3,128,128),f32),pltpu.SemaphoreType.DMA((nb,nb)),pltpu.SemaphoreType.DMA((extra,nb)),pltpu.SemaphoreType.DMA((2,))],
        compiler_params=pltpu.CompilerParams(vmem_limit_bytes=60*2**20),
        name="factor",
    )(*[jnp.asarray(x) for x in t],a,g)

def solve_kernel(nb, chi, clo, phi, plo, s_in, o, yh, yl):
    R=s_in.shape[0]
    for k in range(nb):
        y=s_in[:,k*W:(k+1)*W].astype(f32)
        if k:
            y=y-dot3((yh[:,:k*W],yl[:,:k*W]),(chi[k*W:(k+1)*W,:k*W],clo[k*W:(k+1)*W,:k*W]),NT)
        y=split(y)
        yh[:,k*W:(k+1)*W]=y[0]; yl[:,k*W:(k+1)*W]=y[1]
    for k in reversed(range(nb)):
        sl=slice(k*W,(k+1)*W)
        z=dot3((yh[:,sl],yl[:,sl]),(phi[k],plo[k]),NN)
        if k+1<nb:
            r=slice((k+1)*W,nb*W)
            z=z-dot3((yh[:,r],yl[:,r]),(chi[r,sl],clo[r,sl]),NN)
        x=split(z)
        yh[:,sl]=x[0]; yl[:,sl]=x[1]
        o[:,sl]=x[0]

def solve_call(chi,clo,phi,plo,s):
    n=chi.shape[0]; nb=n//W
    vm=pl.BlockSpec(memory_space=pltpu.VMEM)
    return pl.pallas_call(functools.partial(solve_kernel,nb),out_shape=jax.ShapeDtypeStruct(s.shape,bf),
        in_specs=[vm]*5,out_specs=vm,scratch_shapes=[pltpu.VMEM(s.shape,bf),pltpu.VMEM(s.shape,bf)],
        compiler_params=pltpu.CompilerParams(vmem_limit_bytes=60*2**20),name="solve")(chi,clo,phi,plo,s)

from jax.sharding import PartitionSpec as P

decay_rate = 0.5
damping = 0.1


def shifted(shard, axis, by):
    devices = lax.axis_size(axis)
    return lax.ppermute(shard, axis, [(i, (i + by) % devices) for i in range(devices)])


def per_device(features, previous, gradient):
    layers = lax.axis_size("factor") // 8
    shards = lax.axis_size("dp")
    factor_index = lax.axis_index("factor")
    layer_index = factor_index % layers
    member = factor_index // layers
    block_size = previous.shape[1]
    row_count = block_size // shards
    weight = (1.0 - decay_rate) / (features.shape[0] * shards)
    own_tokens = features[:, 0, :]
    start = lax.axis_index("dp") * row_count
    slot_ids = jnp.arange(2 * layers)
    slot_hot = jnp.where(slot_ids == 2 * layer_index + member % 2, 1.0, 0.0).astype(f32)
    stale = lax.dynamic_slice(previous[0], (start, start), (row_count, row_count))
    partial = weight * jnp.sum(jnp.square(own_tokens.astype(f32))) + decay_rate * jnp.trace(stale)
    traces = lax.psum(partial * slot_hot, ("dp", "factor"))
    input_trace = jnp.sum(jnp.where(slot_ids == 2 * layer_index, traces, 0.0))
    grad_trace = jnp.sum(jnp.where(slot_ids == 2 * layer_index + 1, traces, 0.0))
    pi_ratio = jnp.sqrt(input_trace / grad_trace)
    diag_shift = jnp.where(member % 2 == 0, pi_ratio, 1.0 / pi_ratio) * math.sqrt(damping)

    tokens = lax.all_gather(own_tokens, "dp", axis=0, tiled=True)
    gram = lax.dot_general(tokens, tokens, (((0,), (0,)), ((), ())), preferred_element_type=f32)
    factor = decay_rate * previous[0] + weight * gram
    own_rows = lax.dynamic_slice_in_dim(factor, start, row_count, 0)
    rows = lax.broadcasted_iota(jnp.int32, factor.shape, 0)
    cols = lax.broadcasted_iota(jnp.int32, factor.shape, 1)
    damped = factor + jnp.where(rows == cols, diag_shift, 0.0)

    tile_rows = gradient.shape[2]
    flat = gradient[0].reshape(2 * tile_rows, block_size).astype(f32)
    chi, clo, phi, plo, section_one = factor_call(damped, flat)
    section_one = section_one.reshape(2, tile_rows, block_size)
    moved = lax.all_to_all(section_one, "dp", split_axis=2, concat_axis=1, tiled=True)
    arrived = [shifted(moved[t], "factor", -layers * (2 * t + 1)) for t in range(2)]
    right = jnp.concatenate([a.T for a in arrived], axis=0)
    solved = solve_call(chi, clo, phi, plo, right)
    width = block_size // shards
    back = [shifted(solved[t * width : (t + 1) * width].T, "factor", layers * (2 * t + 1)) for t in range(2)]
    return (own_rows[None], jnp.stack(back)[None])


def solution(mesh):
    placed = (P("dp", "factor", None), P("factor", None, None), P("factor", None, "dp", None))
    return jax.shard_map(
        per_device,
        mesh=mesh,
        in_specs=placed,
        out_specs=(P("factor", "dp", None), P("factor", None, None, "dp")),
        check_vma=False,
    )
```

```python
import math
import jax, jax.numpy as jnp, numpy as np, functools
from jax import lax
from jax.experimental import pallas as pl
from jax.experimental.pallas import tpu as pltpu
W=256

def inv2(a,b,c):
    r = 1.0/(a*c-b*b)
    return c*r, -b*r, a*r

def inv4(p):
    a,b,c = inv2(p[0][0],p[0][1],p[1][1])
    b00,b01,b10,b11 = p[0][2],p[0][3],p[1][2],p[1][3]
    w00=a*b00+b*b10; w01=a*b01+b*b11; w10=b*b00+c*b10; w11=b*b01+c*b11
    s00=p[2][2]-(b00*w00+b10*w10); s01=p[2][3]-(b00*w01+b10*w11); s11=p[3][3]-(b01*w01+b11*w11)
    d00,d01,d11=inv2(s00,s01,s11)
    x00=-(w00*d00+w01*d01); x01=-(w00*d01+w01*d11); x10=-(w10*d00+w11*d01); x11=-(w10*d01+w11*d11)
    t00=a-(x00*w00+x01*w01); t01=b-(x00*w10+x01*w11); t11=c-(x10*w10+x11*w11)
    return [[t00,t01,x00,x01],[t01,t11,x10,x11],[x00,x10,d00,d01],[x01,x11,d01,d11]]

def invq(p,q):
    if q==1: return [[1.0/p[0][0]]]
    if q==2:
        a,b,c=inv2(p[0][0],p[0][1],p[1][1]); return [[a,b],[b,c]]
    return inv4(p)

NN=(((1,),(0,)),((),())); NT=(((1,),(1,)),((),()))
bf=jnp.bfloat16; f32=jnp.float32
def split(x):
    hi=x.astype(bf); return hi,(x-hi.astype(f32)).astype(bf)
def dot3(a,b,dims):
    d=lambda x,y: lax.dot_general(x,y,dims,preferred_element_type=f32)
    return d(a[0],b[0])+(d(a[0],b[1])+d(a[1],b[0]))

def sweep(A, slot, q=4, n=128):
    lane = lax.broadcasted_iota(jnp.int32,(1,n),1)
    for s in range(0,n,q):
        rows=[A[s+i:s+i+1,:] for i in range(q)]
        p=[[jnp.broadcast_to(rows[i][:,s+j:s+j+1],(1,n)) if j>=i else None for j in range(q)] for i in range(q)]
        X=invq(p,q)
        inl=(lane>=s)&(lane<s+q)
        rm=[jnp.where(lane==s+i,1.0,jnp.where(inl,0.0,rows[i])) for i in range(q)]
        nr=[]
        for i in range(q):
            t=X[i][0]*rm[0]
            for j in range(1,q): t=t+X[i][j]*rm[j]
            nr.append(t)
        tiles=[]
        for r in range(0,n,8):
            T=A[r:r+8,:]
            cols=[jnp.broadcast_to(T[:,s+i:s+i+1],(8,n)) for i in range(q)]
            T=jnp.where(inl,0.0,T)
            if r<=s<r+8:
                ri=lax.broadcasted_iota(jnp.int32,(8,1),0)+r
                inr=(ri>=s)&(ri<s+q)
                T=jnp.where(inr,0.0,T)
                cols=[jnp.where(ri==s+i,-1.0,jnp.where(inr,0.0,cols[i])) for i in range(q)]
            for i in range(q): T=T-cols[i]*nr[i]
            tiles.append(T)
        A=jnp.concatenate(tiles,axis=0)
        slot(s//q)
    return A

def tables(nb, extra, slots):
    dst=np.zeros((nb,slots),np.int32); li=np.zeros((nb,slots),np.int32); rj=np.zeros((nb,slots),np.int32)
    dst[:]=nb-1
    for k in range(1,nb):
        t=0
        for j in range(k,nb):
            for i in range(j,nb+extra):
                if (i,j)==(k,k): continue
                dst[k,t]=i*nb+j; li[k,t]=i; rj[k,t]=j; t+=1
        assert t<=slots
    return dst,li,rj

def factor_kernel(nb, extra, interleave, dst_t, li_t, rj_t, a_hbm, g_hbm, shift, chi_hbm, clo_hbm, phi_o, plo_o, s_o,
                  blk, chi, clo, uh, ul, ch, cl, half, asem, gsem, osem):
    nr=nb+extra
    first=[]; rest=[]
    for j in range(nb):
        for i in range(j,nb):
            c=pltpu.make_async_copy(a_hbm.at[i*nb+j], blk.at[i*nb+j], asem.at[i,j])
            (first if (i,j)==(0,0) else rest).append(c)
        for e in range(extra):
            rest.append(pltpu.make_async_copy(g_hbm.at[pl.ds(e*W,W),pl.ds(j*W,W)], blk.at[(nb+e)*nb+j], gsem.at[e,j]))
    for c in first+rest: c.start()
    for c in first: c.wait()
    eye=jnp.where(lax.broadcasted_iota(jnp.int32,(128,128),0)==lax.broadcasted_iota(jnp.int32,(128,128),1),shift[0:1,0:1],0.0)

    def tile(k,t):
        d=dst_t[k,t]; i=li_t[k,t]; j=rj_t[k,t]
        blk[d]=blk[d]-dot3((ch[i],cl[i]),(uh[j],ul[j]),NT)

    def step(k,_):
        kk=k*nb+k
        half[0]=blk[kk,:128,:128]+eye
        def hbody(h,_):
            fn=(lambda s: tile(k,h*32+s)) if interleave else (lambda s:None)
            p=sweep(half[h],fn)
            half[h]=p
            @pl.when((k==0)&(h==0))
            def _():
                for c in rest: c.wait()
            @pl.when(h==0)
            def _():
                d21=split(blk[kk,128:,:128])
                w=dot3(d21,split(p),NN)
                half[2]=w
                half[1]=(blk[kk,128:,128:]+eye)-dot3(split(w),d21,NT)
            return 0
        lax.fori_loop(0,2,hbody,0)
        p2=split(half[1]); w=half[2]
        x21=-dot3(p2,split(w),NN)
        wt=split(w.T)
        x11=half[0]-dot3(wt,split(x21),NN)
        x12=x21.T
        top=jnp.concatenate([x11,x12],axis=1)
        bot=jnp.concatenate([x21,half[1]],axis=1)
        P=split(jnp.concatenate([top,bot],axis=0))
        phi_o[k]=P[0]; plo_o[k]=P[1]
        if not interleave:
            def lp(t,_):
                tile(k,t); return 0
            lax.fori_loop(0,jnp.where(k==0,0,jnp.int32(64)),lp,0)
        def cbody(i,_):
            u=split(blk[i*nb+k])
            uh[i]=u[0]; ul[i]=u[1]
            c=dot3(u,(phi_o[k],plo_o[k]),NN)
            blk[i*nb+k]=c
            cs=split(c)
            ch[i]=cs[0]; cl[i]=cs[1]
            return 0
        lax.fori_loop(k+1,nr,cbody,0)
        def st(i,_):
            r=pl.ds(pl.multiple_of(i*W,W),W); c=pl.ds(pl.multiple_of(k*W,W),W)
            chi[r,c]=ch[i]; clo[r,c]=cl[i]
            return 0
        lax.fori_loop(k+1,nb,st,0)
        @pl.when(k+1<nb)
        def _():
            d=(k+1)*nb+k+1
            blk[d]=blk[d]-dot3((ch[k+1],cl[k+1]),(uh[k+1],ul[k+1]),NT)
        return 0
    lax.fori_loop(0,nb,step,0)
    o1=pltpu.make_async_copy(chi,chi_hbm,osem.at[0]); o2=pltpu.make_async_copy(clo,clo_hbm,osem.at[1])
    o1.start(); o2.start()
    for k in reversed(range(nb)):
        for e in range(extra):
            z=blk[(nb+e)*nb+k]
            for i in range(k+1,nb):
                cc=(chi[i*W:(i+1)*W,k*W:(k+1)*W],clo[i*W:(i+1)*W,k*W:(k+1)*W])
                xi=(blk_x(uh,ch,e,nb)[i], blk_x(ul,cl,e,nb)[i])
                z=z-dot3(xi,cc,NN)
            x=split(z)
            blk_x(uh,ch,e,nb)[k]=x[0]; blk_x(ul,cl,e,nb)[k]=x[1]
            s_o[k,e]=z.T.astype(bf)
    o1.wait(); o2.wait()
def blk_x(u,c,e,nb): return u if e==0 else c

def factor_call(a,g,shift,interleave=True):
    n=g.shape[1]; nb=n//W; extra=g.shape[0]//W
    t=tables(nb,extra,64)
    sm=pl.BlockSpec(memory_space=pltpu.SMEM); an=pl.BlockSpec(memory_space=pl.ANY); vm=pl.BlockSpec(memory_space=pltpu.VMEM)
    return pl.pallas_call(
        functools.partial(factor_kernel,nb,extra,interleave),
        out_shape=(jax.ShapeDtypeStruct((n,n),bf),jax.ShapeDtypeStruct((n,n),bf),jax.ShapeDtypeStruct((nb,W,W),bf),jax.ShapeDtypeStruct((nb,W,W),bf),jax.ShapeDtypeStruct((nb,extra,W,W),bf)),
        in_specs=[sm,sm,sm,an,an,vm], out_specs=(an,an,vm,vm,vm),
        scratch_shapes=[pltpu.VMEM(((nb+extra)*nb,W,W),f32),pltpu.VMEM((n,n),bf),pltpu.VMEM((n,n),bf),
            pltpu.VMEM((nb+extra,W,W),bf),pltpu.VMEM((nb+extra,W,W),bf),pltpu.VMEM((nb+extra,W,W),bf),pltpu.VMEM((nb+extra,W,W),bf),
            pltpu.VMEM((3,128,128),f32),pltpu.SemaphoreType.DMA((nb,nb)),pltpu.SemaphoreType.DMA((extra,nb)),pltpu.SemaphoreType.DMA((2,))],
        compiler_params=pltpu.CompilerParams(vmem_limit_bytes=60*2**20),
        name="factor",
    )(*[jnp.asarray(x) for x in t],a,g,shift)


from jax.sharding import PartitionSpec as P

decay_rate = 0.5
damping = 0.1

MESH = pl.DeviceIdType.MESH


def gather_kernel(dec, weight, damp, layers, own, prev, blocks, c_o, ft, acc, diag, part, tr1, tr2, zs, zr, t1s, t1r, t2s, t2r, psem, osem, lsem):
    dp = lax.axis_index("dp")
    f = lax.axis_index("factor")
    nb = 8
    z, y = dp // 4, dp % 4
    oz = 1 - z
    up, down = z * 4 + (y + 1) % 4, z * 4 + (y + 3) % 4
    member, layer = f // layers, f % layers
    far = z * 4 + (y + 2) % 4
    other, oup, odown, ofar = oz * 4 + y, oz * 4 + (y + 1) % 4, oz * 4 + (y + 3) % 4, oz * 4 + (y + 2) % 4

    loads = {}
    for i in range(nb):
        for j in range(i + 1):
            loads[i, j] = pltpu.make_async_copy(
                prev.at[0, pl.ds(i * W, W), pl.ds(j * W, W)], acc.at[i * nb + j], psem.at[i, j])
    row = pl.ds(pl.multiple_of(dp * W, W), W)
    dcopy = pltpu.make_async_copy(prev.at[0, row, row], diag, lsem.at[0])
    mine = pltpu.make_async_copy(own, ft.at[dp], lsem.at[1])
    dcopy.start()
    mine.start()

    barrier = pltpu.get_barrier_semaphore()
    for off in range(1, 8):
        pl.semaphore_signal(barrier, inc=1, device_id=((dp + off) % 8, f), device_id_type=MESH)
        pl.semaphore_signal(barrier, inc=1, device_id=(dp, ((member + off) % 8) * layers + layer), device_id_type=MESH)
    pl.semaphore_wait(barrier, 14)

    CH = zs.shape[0]
    rows = ft.shape[1] // CH
    half = rows // 2

    def send(kind, c, src, slot, to, lo, n):
        r = pl.ds(c * rows + lo, n)
        return pltpu.make_async_remote_copy(
            src_ref=src.at[r], dst_ref=ft.at[slot, r], send_sem=zs.at[c, kind], recv_sem=zr.at[c, kind],
            device_id=(to, f), device_id_type=MESH)

    cp = {}
    for c in range(CH):
        cp[0, c] = send(0, c, own, dp, other, 0, rows)
        cp[1, c] = send(1, c, own, dp, up, 0, rows)
        cp[2, c] = send(2, c, own, dp, down, 0, rows)
        cp[3, c] = send(3, c, ft.at[down], down, up, 0, half)
        cp[4, c] = send(4, c, ft.at[up], up, down, half, half)
        cp[5, c] = send(5, c, ft.at[other], other, up, 0, rows)
        cp[6, c] = send(6, c, ft.at[other], other, down, 0, rows)
        cp[7, c] = send(7, c, ft.at[odown], odown, up, 0, half)
        cp[8, c] = send(8, c, ft.at[oup], oup, down, half, half)
    for c in range(CH):
        for kind in range(3):
            cp[kind, c].start()

    dcopy.wait()
    ii = lax.broadcasted_iota(jnp.int32, (W, W), 0)
    jj = lax.broadcasted_iota(jnp.int32, (W, W), 1)
    tr = jnp.sum(jnp.where(ii == jj, diag[...], 0.0))
    xs = own[...].astype(f32)
    share = dec * tr + weight * jnp.sum(xs * xs)
    part[0] = jnp.full((8, 128), share, f32)
    tr1[dp] = part[0]
    c1 = [pltpu.make_async_remote_copy(
        src_ref=part.at[0], dst_ref=tr1.at[dp], send_sem=t1s.at[off], recv_sem=t1r.at[off],
        device_id=((dp + off) % 8, f), device_id_type=MESH) for off in range(1, 8)]
    for x in c1:
        x.start()
    for x in loads.values():
        x.start()
    for x in c1:
        x.wait()
    total = tr1[0]
    for i in range(1, 8):
        total = total + tr1[i]
    part[1] = total
    tr2[member] = total
    c2 = [pltpu.make_async_remote_copy(
        src_ref=part.at[1], dst_ref=tr2.at[member], send_sem=t2s.at[off], recv_sem=t2r.at[off],
        device_id=(dp, ((member + off) % 8) * layers + layer), device_id_type=MESH) for off in range(1, 8)]
    for x in c2:
        x.start()
    for x in loads.values():
        x.wait()
    mine.wait()

    per = nb // CH

    def tiles(c, slots, first):
        for i in range(c * per, (c + 1) * per):
            def body(j, _):
                d = None
                for s in slots:
                    t = lax.dot_general(ft[s, i * W:(i + 1) * W, :], ft[s, pl.ds(pl.multiple_of(j * W, W), W), :], NT, preferred_element_type=f32)
                    d = t if d is None else d + t
                old = acc[i * nb + j]
                acc[i * nb + j] = (dec * old if first else old) + weight * d
                return 0
            lax.fori_loop(0, i + 1, body, 0)

    for c in range(CH):
        cp[1, c].wait_recv()
        cp[3, c].start()
        cp[2, c].wait_recv()
        cp[4, c].start()
        cp[0, c].wait_recv()
        cp[5, c].start()
        cp[6, c].start()
        tiles(c, [dp, down, up, other], True)
    for x in c2:
        x.wait()
    s_in = tr2[0] + tr2[2] + tr2[4] + tr2[6]
    s_out = tr2[1] + tr2[3] + tr2[5] + tr2[7]
    ratio = jnp.sqrt(s_in / s_out)
    even = (jnp.full((8, 128), member, jnp.int32) % 2) == 0
    c_o[...] = jnp.where(even, ratio, 1.0 / ratio) * damp
    for c in range(CH):
        cp[5, c].wait_recv()
        cp[7, c].start()
        cp[6, c].wait_recv()
        cp[8, c].start()
        cp[3, c].wait_recv()
        cp[4, c].wait_recv()
        tiles(c, [odown, oup, far], False)
    outs = []
    for c in range(CH):
        cp[7, c].wait_recv()
        cp[8, c].wait_recv()
        tiles(c, [ofar], False)
        for i in range(c * per, (c + 1) * per):
            for j in range(i + 1):
                o = pltpu.make_async_copy(acc.at[i * nb + j], blocks.at[i * nb + j], osem.at[i, j])
                o.start()
                outs.append(o)
    for x in cp.values():
        x.wait_send()
    for o in outs:
        o.wait()


def gather_call(own, prev, layers, weight):
    n, w = own.shape
    nb = n // W
    CH = 4
    an = pl.BlockSpec(memory_space=pl.ANY)
    vm = pl.BlockSpec(memory_space=pltpu.VMEM)
    D = pltpu.SemaphoreType.DMA
    return pl.pallas_call(
        functools.partial(gather_kernel, decay_rate, weight, math.sqrt(damping), layers),
        out_shape=(jax.ShapeDtypeStruct((nb * nb, W, W), f32), jax.ShapeDtypeStruct((8, 128), f32)),
        in_specs=[vm, an], out_specs=(an, vm),
        scratch_shapes=[pltpu.VMEM((8, n, w), bf), pltpu.VMEM((nb * nb, W, W), f32), pltpu.VMEM((W, W), f32),
                        pltpu.VMEM((2, 8, 128), f32), pltpu.VMEM((8, 8, 128), f32), pltpu.VMEM((8, 8, 128), f32),
                        D((CH, 9)), D((CH, 9)), D((8,)), D((8,)), D((8,)), D((8,)), D((nb, nb)), D((nb, nb)), D((2,))],
        compiler_params=pltpu.CompilerParams(vmem_limit_bytes=56 * 2**20, collective_id=0, has_side_effects=True),
        cost_estimate=pl.CostEstimate(flops=10**10, bytes_accessed=3 * 10**7, transcendentals=0),
        name="gather_gram",
    )(own, prev)


def exchange_kernel(layers, s, blocks, chi_h, clo_h, phi_h, plo_h, out, rows_o,
                    chi, clo, phi, plo, arr, yh, yl, xb, rb, ss, sr, bs, br, csem, psem, rsem):
    dp = lax.axis_index("dp")
    f = lax.axis_index("factor")
    nf = lax.axis_size("factor")
    nb = chi.shape[0] // W
    to = [lax.rem(f + nf - layers * (2 * t + 1), nf) for t in range(2)]
    frm = [lax.rem(f + layers * (2 * t + 1), nf) for t in range(2)]
    barrier = pltpu.get_barrier_semaphore()
    for t in range(2):
        for off in range(8):
            pl.semaphore_signal(barrier, inc=1, device_id=(lax.rem(dp + off, 8), frm[t]), device_id_type=MESH)
            pl.semaphore_signal(barrier, inc=1, device_id=(lax.rem(dp + off, 8), to[t]), device_id_type=MESH)
    pl.semaphore_wait(barrier, 32)

    sends = []
    for off in range(8):
        for t in range(2):
            peer = lax.rem(dp + off, 8)
            x = pltpu.make_async_remote_copy(
                src_ref=s.at[peer, t], dst_ref=arr.at[dp, t], send_sem=ss.at[off, t], recv_sem=sr.at[dp, t],
                device_id=(peer, to[t]), device_id_type=MESH)
            x.start()
            sends.append(x)
    lp = [pltpu.make_async_copy(phi_h, phi, psem.at[0]), pltpu.make_async_copy(plo_h, plo, psem.at[1])]
    lc = {}
    for k in range(1, nb):
        a, b = slice(k * W, (k + 1) * W), slice(0, k * W)
        lc[k] = [pltpu.make_async_copy(chi_h.at[a, b], chi.at[a, b], csem.at[k, 0]),
                 pltpu.make_async_copy(clo_h.at[a, b], clo.at[a, b], csem.at[k, 1])]
    for k in range(1, nb):
        for x in lc[k]:
            x.start()
    for x in lp:
        x.start()
    lr = []
    for j in range(nb):
        idx = jnp.maximum(dp, j) * nb + jnp.minimum(dp, j)
        x = pltpu.make_async_copy(blocks.at[idx], rb.at[j], rsem.at[j])
        x.start()
        lr.append(x)
    for j in range(nb):
        lr[j].wait()
        v = rb[j]
        low = jnp.full((W, W), dp, jnp.int32) >= j
        rows_o[:, j * W:(j + 1) * W] = jnp.where(low, v, v.T)

    for k in range(nb):
        for t in range(2):
            pltpu.make_async_remote_copy(
                src_ref=s.at[k, t], dst_ref=arr.at[k, t], send_sem=ss.at[0, t], recv_sem=sr.at[k, t],
                device_id=(dp, to[t]), device_id_type=MESH).wait_recv()
        y = jnp.concatenate([arr[k, 0], arr[k, 1]], axis=0).astype(f32)
        if k:
            for x in lc[k]:
                x.wait()
            y = y - dot3((yh[:, :k * W], yl[:, :k * W]), (chi[k * W:(k + 1) * W, :k * W], clo[k * W:(k + 1) * W, :k * W]), NT)
        y = split(y)
        yh[:, k * W:(k + 1) * W] = y[0]
        yl[:, k * W:(k + 1) * W] = y[1]
    for x in lp:
        x.wait()
    backs = []
    for k in reversed(range(nb)):
        sl = slice(k * W, (k + 1) * W)
        zk = dot3((yh[:, sl], yl[:, sl]), (phi[k], plo[k]), NN)
        if k + 1 < nb:
            r = slice((k + 1) * W, nb * W)
            zk = zk - dot3((yh[:, r], yl[:, r]), (chi[r, sl], clo[r, sl]), NN)
        x = split(zk)
        yh[:, sl] = x[0]
        yl[:, sl] = x[1]
        for t in range(2):
            xb[k, t] = zk[t * W:(t + 1) * W].T.astype(bf)
            b = pltpu.make_async_remote_copy(
                src_ref=xb.at[k, t], dst_ref=out.at[t, pl.ds(k * W, W)], send_sem=bs.at[k, t], recv_sem=br.at[k, t],
                device_id=(dp, frm[t]), device_id_type=MESH)
            b.start()
            backs.append(b)
    for x in sends:
        x.wait_send()
    for b in backs:
        b.wait()


def exchange_call(s, blocks, chi, clo, phi, plo, layers):
    n = chi.shape[0]
    nb = n // W
    an = pl.BlockSpec(memory_space=pl.ANY)
    vm = pl.BlockSpec(memory_space=pltpu.VMEM)
    D = pltpu.SemaphoreType.DMA
    V = pltpu.VMEM
    return pl.pallas_call(
        functools.partial(exchange_kernel, layers),
        out_shape=(jax.ShapeDtypeStruct((2, n, W), bf), jax.ShapeDtypeStruct((W, n), f32)),
        in_specs=[vm] + [an] * 5, out_specs=(an, vm),
        scratch_shapes=[V((n, n), bf), V((n, n), bf), V((nb, W, W), bf), V((nb, W, W), bf), V((nb, 2, W, W), bf),
                        V((2 * W, n), bf), V((2 * W, n), bf), V((nb, 2, W, W), bf), V((nb, W, W), f32),
                        D((8, 2)), D((8, 2)), D((nb, 2)), D((nb, 2)), D((nb, 2)), D((2,)), D((nb,))],
        compiler_params=pltpu.CompilerParams(vmem_limit_bytes=56 * 2**20, collective_id=1, has_side_effects=True),
        cost_estimate=pl.CostEstimate(flops=13 * 10**9, bytes_accessed=3 * 10**7, transcendentals=0),
        name="exchange_solve",
    )(s, blocks, chi, clo, phi, plo)


def per_device(features, previous, gradient):
    layers = lax.axis_size("factor") // 8
    shards = lax.axis_size("dp")
    block_size = previous.shape[1]
    weight = (1.0 - decay_rate) / (features.shape[0] * shards)
    blocks, shift = gather_call(features[:, 0, :].T, previous, layers, weight)
    tile_rows = gradient.shape[2]
    flat = gradient[0].reshape(2 * tile_rows, block_size).astype(f32)
    chi, clo, phi, plo, section_one = factor_call(blocks, flat, shift)
    result, own_rows = exchange_call(section_one, blocks, chi, clo, phi, plo, layers)
    return (own_rows[None], result[None])


def solution(mesh):
    placed = (P("dp", "factor", None), P("factor", None, None), P("factor", None, "dp", None))
    return jax.shard_map(
        per_device,
        mesh=mesh,
        in_specs=placed,
        out_specs=(P("factor", "dp", None), P("factor", None, None, "dp")),
        check_vma=False,
    )
```

```python
import math
import jax, jax.numpy as jnp, numpy as np, functools
from jax import lax
from jax.experimental import pallas as pl
from jax.experimental.pallas import tpu as pltpu
W=256

def inv2(a,b,c):
    r = 1.0/(a*c-b*b)
    return c*r, -b*r, a*r

def inv4(p):
    a,b,c = inv2(p[0][0],p[0][1],p[1][1])
    b00,b01,b10,b11 = p[0][2],p[0][3],p[1][2],p[1][3]
    w00=a*b00+b*b10; w01=a*b01+b*b11; w10=b*b00+c*b10; w11=b*b01+c*b11
    s00=p[2][2]-(b00*w00+b10*w10); s01=p[2][3]-(b00*w01+b10*w11); s11=p[3][3]-(b01*w01+b11*w11)
    d00,d01,d11=inv2(s00,s01,s11)
    x00=-(w00*d00+w01*d01); x01=-(w00*d01+w01*d11); x10=-(w10*d00+w11*d01); x11=-(w10*d01+w11*d11)
    t00=a-(x00*w00+x01*w01); t01=b-(x00*w10+x01*w11); t11=c-(x10*w10+x11*w11)
    return [[t00,t01,x00,x01],[t01,t11,x10,x11],[x00,x10,d00,d01],[x01,x11,d01,d11]]

def invq(p,q):
    if q==1: return [[1.0/p[0][0]]]
    if q==2:
        a,b,c=inv2(p[0][0],p[0][1],p[1][1]); return [[a,b],[b,c]]
    return inv4(p)

NN=(((1,),(0,)),((),())); NT=(((1,),(1,)),((),()))
bf=jnp.bfloat16; f32=jnp.float32
def split(x):
    hi=x.astype(bf); return hi,(x-hi.astype(f32)).astype(bf)
def dot3(a,b,dims):
    d=lambda x,y: lax.dot_general(x,y,dims,preferred_element_type=f32)
    return d(a[0],b[0])+(d(a[0],b[1])+d(a[1],b[0]))

def sweep(A, slot, q=4, n=128):
    lane = lax.broadcasted_iota(jnp.int32,(1,n),1)
    for s in range(0,n,q):
        rows=[A[s+i:s+i+1,:] for i in range(q)]
        p=[[jnp.broadcast_to(rows[i][:,s+j:s+j+1],(1,n)) if j>=i else None for j in range(q)] for i in range(q)]
        X=invq(p,q)
        inl=(lane>=s)&(lane<s+q)
        rm=[jnp.where(lane==s+i,1.0,jnp.where(inl,0.0,rows[i])) for i in range(q)]
        nr=[]
        for i in range(q):
            t=X[i][0]*rm[0]
            for j in range(1,q): t=t+X[i][j]*rm[j]
            nr.append(t)
        tiles=[]
        for r in range(0,n,8):
            T=A[r:r+8,:]
            cols=[jnp.broadcast_to(T[:,s+i:s+i+1],(8,n)) for i in range(q)]
            T=jnp.where(inl,0.0,T)
            if r<=s<r+8:
                ri=lax.broadcasted_iota(jnp.int32,(8,1),0)+r
                inr=(ri>=s)&(ri<s+q)
                T=jnp.where(inr,0.0,T)
                cols=[jnp.where(ri==s+i,-1.0,jnp.where(inr,0.0,cols[i])) for i in range(q)]
            for i in range(q): T=T-cols[i]*nr[i]
            tiles.append(T)
        A=jnp.concatenate(tiles,axis=0)
        slot(s//q)
    return A

def tables(nb, extra, slots):
    dst=np.zeros((nb,slots),np.int32); li=np.zeros((nb,slots),np.int32); rj=np.zeros((nb,slots),np.int32)
    dst[:]=nb-1
    for k in range(1,nb):
        t=0
        for j in range(k,nb):
            for i in range(j,nb+extra):
                if (i,j)==(k,k): continue
                dst[k,t]=i*nb+j; li[k,t]=i; rj[k,t]=j; t+=1
        assert t<=slots
    return dst,li,rj

def factor_kernel(nb, extra, interleave, dst_t, li_t, rj_t, a_hbm, g_hbm, shift, chi_hbm, clo_hbm, phi_o, plo_o, s_o,
                  blk, gst, chi, clo, uh, ul, ch, cl, half, asem, gsem, osem):
    nr=nb+extra
    cslots=nr-2
    first=[]; rest=[]
    for j in range(nb):
        for i in range(j,nb):
            c=pltpu.make_async_copy(a_hbm.at[i*nb+j], blk.at[i*nb+j], asem.at[i,j])
            (first if (i,j)==(0,0) else rest).append(c)
    rest.append(pltpu.make_async_copy(g_hbm, gst, gsem.at[0]))
    for c in first+rest: c.start()
    for c in first: c.wait()
    eye=jnp.where(lax.broadcasted_iota(jnp.int32,(128,128),0)==lax.broadcasted_iota(jnp.int32,(128,128),1),shift[0:1,0:1],0.0)

    def tile(k,t):
        d=dst_t[k,t]; i=li_t[k,t]; j=rj_t[k,t]
        blk[d]=blk[d]-dot3((ch[i],cl[i]),(uh[j],ul[j]),NT)

    def panel(i,k):
        u=split(blk[i*nb+k])
        uh[i]=u[0]; ul[i]=u[1]
        c=split(dot3(u,(phi_o[k],plo_o[k]),NN))
        ch[i]=c[0]; cl[i]=c[1]
        r=pl.ds(pl.multiple_of(i*W,W),W); cc=pl.ds(pl.multiple_of(k*W,W),W)
        chi[r,cc]=c[0]; clo[r,cc]=c[1]

    def step(k,_):
        kk=k*nb+k
        kp=jnp.maximum(k-1,0)
        def slot(h,s):
            if not interleave: return
            if h==0 and s<cslots: panel(jnp.minimum(k+1+s,nr-1),kp)
            else: tile(k,h*32+s-cslots)
        p1=sweep(blk[kk,:128,:128]+eye,lambda s: slot(0,s))
        half[0]=p1
        @pl.when(k==0)
        def _():
            for c in rest: c.wait()
            for j in range(nb):
                for e in range(extra):
                    blk[(nb+e)*nb+j]=gst[e*W:(e+1)*W,j*W:(j+1)*W].astype(f32)
        d21=split(blk[kk,128:,:128])
        w=dot3(d21,split(half[0]),NN)
        sw=split(w)
        half[2]=w
        p2v=sweep((blk[kk,128:,128:]+eye)-dot3(sw,d21,NT),lambda s: slot(1,s))
        p2=split(p2v); w=half[2]
        x21=-dot3(p2,split(w),NN)
        x11=half[0]-dot3(split(w.T),split(x21),NN)
        top=jnp.concatenate([x11,x21.T],axis=1)
        bot=jnp.concatenate([x21,p2v],axis=1)
        P=split(jnp.concatenate([top,bot],axis=0))
        phi_o[k]=P[0]; plo_o[k]=P[1]
        if not interleave:
            def lp(t,_):
                tile(k,t); return 0
            lax.fori_loop(0,jnp.where(k==0,0,jnp.int32(64)),lp,0)
            def lc(i,_):
                panel(i,k); return 0
            lax.fori_loop(k+2,nr,lc,0)
        panel(k+1,k)
        @pl.when(k+1<nb)
        def _():
            d=(k+1)*nb+k+1
            blk[d]=blk[d]-dot3((ch[k+1],cl[k+1]),(uh[k+1],ul[k+1]),NT)
        return 0
    lax.fori_loop(0,nb,step,0)
    o1=pltpu.make_async_copy(chi.at[pl.ds(0,nb*W)],chi_hbm,osem.at[0]); o2=pltpu.make_async_copy(clo.at[pl.ds(0,nb*W)],clo_hbm,osem.at[1])
    o1.start(); o2.start()
    for i in range(nb+1,nr): panel(i,nb-1)
    er=slice(nb*W,nr*W)
    for k in reversed(range(nb)):
        sl=slice(k*W,(k+1)*W)
        z=chi[er,sl].astype(f32)+clo[er,sl].astype(f32)
        if k+1<nb:
            b=slice((k+1)*W,nb*W)
            z=z-dot3((chi[er,b],clo[er,b]),(chi[b,sl],clo[b,sl]),NN)
        x=split(z)
        chi[er,sl]=x[0]; clo[er,sl]=x[1]
        for e in range(extra): s_o[k,e]=z[e*W:(e+1)*W].T.astype(bf)
    o1.wait(); o2.wait()
def factor_call(a,g,shift,interleave=True):
    n=g.shape[1]; nb=n//W; extra=g.shape[0]//W
    t=tables(nb,extra,64-(nb+extra-2))
    sm=pl.BlockSpec(memory_space=pltpu.SMEM); an=pl.BlockSpec(memory_space=pl.ANY); vm=pl.BlockSpec(memory_space=pltpu.VMEM)
    return pl.pallas_call(
        functools.partial(factor_kernel,nb,extra,interleave),
        out_shape=(jax.ShapeDtypeStruct((n,n),bf),jax.ShapeDtypeStruct((n,n),bf),jax.ShapeDtypeStruct((nb,W,W),bf),jax.ShapeDtypeStruct((nb,W,W),bf),jax.ShapeDtypeStruct((nb,extra,W,W),bf)),
        in_specs=[sm,sm,sm,an,an,vm], out_specs=(an,an,vm,vm,vm),
        scratch_shapes=[pltpu.VMEM(((nb+extra)*nb,W,W),f32),pltpu.VMEM((extra*W,n),bf),pltpu.VMEM((n+extra*W,n),bf),pltpu.VMEM((n+extra*W,n),bf),
            pltpu.VMEM((nb+extra,W,W),bf),pltpu.VMEM((nb+extra,W,W),bf),pltpu.VMEM((nb+extra,W,W),bf),pltpu.VMEM((nb+extra,W,W),bf),
            pltpu.VMEM((3,128,128),f32),pltpu.SemaphoreType.DMA((nb,nb)),pltpu.SemaphoreType.DMA((1,)),pltpu.SemaphoreType.DMA((2,))],
        compiler_params=pltpu.CompilerParams(vmem_limit_bytes=60*2**20),
        name="factor",
    )(*[jnp.asarray(x) for x in t],a,g,shift)


from jax.sharding import PartitionSpec as P

decay_rate = 0.5
damping = 0.1

MESH = pl.DeviceIdType.MESH


def gather_kernel(dec, weight, damp, layers, own, prev, blocks, c_o, ft, acc, diag, part, tr1, tr2, zs, zr, t1s, t1r, t2s, t2r, psem, osem, lsem):
    dp = lax.axis_index("dp")
    f = lax.axis_index("factor")
    nb = 8
    z, y = dp // 4, dp % 4
    oz = 1 - z
    up, down = z * 4 + (y + 1) % 4, z * 4 + (y + 3) % 4
    member, layer = f // layers, f % layers
    far = z * 4 + (y + 2) % 4
    other, oup, odown, ofar = oz * 4 + y, oz * 4 + (y + 1) % 4, oz * 4 + (y + 3) % 4, oz * 4 + (y + 2) % 4

    loads = {}
    for i in range(nb):
        for j in range(i + 1):
            loads[i, j] = pltpu.make_async_copy(
                prev.at[0, pl.ds(i * W, W), pl.ds(j * W, W)], acc.at[i * nb + j], psem.at[i, j])
    row = pl.ds(pl.multiple_of(dp * W, W), W)
    dcopy = pltpu.make_async_copy(prev.at[0, row, row], diag, lsem.at[0])
    mine = pltpu.make_async_copy(own, ft.at[dp], lsem.at[1])
    dcopy.start()
    mine.start()

    barrier = pltpu.get_barrier_semaphore()
    for off in range(1, 8):
        pl.semaphore_signal(barrier, inc=1, device_id=((dp + off) % 8, f), device_id_type=MESH)
        pl.semaphore_signal(barrier, inc=1, device_id=(dp, ((member + off) % 8) * layers + layer), device_id_type=MESH)
    pl.semaphore_wait(barrier, 14)

    CH = zs.shape[0]
    rows = ft.shape[1] // CH
    half = rows // 2

    def send(kind, c, src, slot, to, lo, n):
        r = pl.ds(c * rows + lo, n)
        return pltpu.make_async_remote_copy(
            src_ref=src.at[r], dst_ref=ft.at[slot, r], send_sem=zs.at[c, kind], recv_sem=zr.at[c, kind],
            device_id=(to, f), device_id_type=MESH)

    cp = {}
    for c in range(CH):
        cp[0, c] = send(0, c, own, dp, other, 0, rows)
        cp[1, c] = send(1, c, own, dp, up, 0, rows)
        cp[2, c] = send(2, c, own, dp, down, 0, rows)
        cp[3, c] = send(3, c, ft.at[down], down, up, 0, half)
        cp[4, c] = send(4, c, ft.at[up], up, down, half, half)
        cp[5, c] = send(5, c, ft.at[other], other, up, 0, half)
        cp[6, c] = send(6, c, ft.at[other], other, down, half, half)
        cp[7, c] = send(7, c, ft.at[odown], odown, up, 0, half)
        cp[8, c] = send(8, c, ft.at[oup], oup, down, half, half)
        cp[9, c] = send(9, c, ft.at[down], down, other, half, half)
        cp[10, c] = send(10, c, ft.at[up], up, other, 0, half)
    for c in range(CH):
        for kind in range(3):
            cp[kind, c].start()

    dcopy.wait()
    ii = lax.broadcasted_iota(jnp.int32, (W, W), 0)
    jj = lax.broadcasted_iota(jnp.int32, (W, W), 1)
    tr = jnp.sum(jnp.where(ii == jj, diag[...], 0.0))
    xs = own[...].astype(f32)
    share = dec * tr + weight * jnp.sum(xs * xs)
    part[0] = jnp.full((8, 128), share, f32)
    tr1[dp] = part[0]
    c1 = [pltpu.make_async_remote_copy(
        src_ref=part.at[0], dst_ref=tr1.at[dp], send_sem=t1s.at[off], recv_sem=t1r.at[off],
        device_id=((dp + off) % 8, f), device_id_type=MESH) for off in range(1, 8)]
    for x in c1:
        x.start()
    for x in loads.values():
        x.start()
    for x in c1:
        x.wait()
    total = tr1[0]
    for i in range(1, 8):
        total = total + tr1[i]
    part[1] = total
    tr2[member] = total
    c2 = [pltpu.make_async_remote_copy(
        src_ref=part.at[1], dst_ref=tr2.at[member], send_sem=t2s.at[off], recv_sem=t2r.at[off],
        device_id=(dp, ((member + off) % 8) * layers + layer), device_id_type=MESH) for off in range(1, 8)]
    for x in c2:
        x.start()

    per = nb // CH

    def tiles(c, slots, first):
        for i in range(c * per, (c + 1) * per):
            def body(j, _):
                d = None
                for s in slots:
                    t = lax.dot_general(ft[s, i * W:(i + 1) * W, :], ft[s, pl.ds(pl.multiple_of(j * W, W), W), :], NT, preferred_element_type=f32)
                    d = t if d is None else d + t
                old = acc[i * nb + j]
                acc[i * nb + j] = (dec * old if first else old) + weight * d
                return 0
            lax.fori_loop(0, i + 1, body, 0)

    for c in range(CH):
        cp[1, c].wait_recv()
        cp[3, c].start()
        cp[9, c].start()
        cp[2, c].wait_recv()
        cp[4, c].start()
        cp[10, c].start()
        cp[0, c].wait_recv()
        cp[5, c].start()
        cp[6, c].start()
    for x in loads.values():
        x.wait()
    mine.wait()
    for c in range(CH):
        tiles(c, [dp, down, up, other], True)
    for x in c2:
        x.wait()
    s_in = tr2[0] + tr2[2] + tr2[4] + tr2[6]
    s_out = tr2[1] + tr2[3] + tr2[5] + tr2[7]
    ratio = jnp.sqrt(s_in / s_out)
    even = (jnp.full((8, 128), member, jnp.int32) % 2) == 0
    c_o[...] = jnp.where(even, ratio, 1.0 / ratio) * damp
    for c in range(CH):
        cp[5, c].wait_recv()
        cp[7, c].start()
        cp[6, c].wait_recv()
        cp[8, c].start()
    for c in range(CH):
        for kind in (3, 4, 9, 10):
            cp[kind, c].wait_recv()
        tiles(c, [odown, oup, far], False)
    outs = []
    for c in range(CH):
        cp[7, c].wait_recv()
        cp[8, c].wait_recv()
        tiles(c, [ofar], False)
        for i in range(c * per, (c + 1) * per):
            for j in range(i + 1):
                o = pltpu.make_async_copy(acc.at[i * nb + j], blocks.at[i * nb + j], osem.at[i, j])
                o.start()
                outs.append(o)
    for x in cp.values():
        x.wait_send()
    for o in outs:
        o.wait()


def gather_call(own, prev, layers, weight):
    n, w = own.shape
    nb = n // W
    CH = 4
    an = pl.BlockSpec(memory_space=pl.ANY)
    vm = pl.BlockSpec(memory_space=pltpu.VMEM)
    D = pltpu.SemaphoreType.DMA
    return pl.pallas_call(
        functools.partial(gather_kernel, decay_rate, weight, math.sqrt(damping), layers),
        out_shape=(jax.ShapeDtypeStruct((nb * nb, W, W), f32), jax.ShapeDtypeStruct((8, 128), f32)),
        in_specs=[vm, an], out_specs=(an, vm),
        scratch_shapes=[pltpu.VMEM((8, n, w), bf), pltpu.VMEM((nb * nb, W, W), f32), pltpu.VMEM((W, W), f32),
                        pltpu.VMEM((2, 8, 128), f32), pltpu.VMEM((8, 8, 128), f32), pltpu.VMEM((8, 8, 128), f32),
                        D((CH, 11)), D((CH, 11)), D((8,)), D((8,)), D((8,)), D((8,)), D((nb, nb)), D((nb, nb)), D((2,))],
        compiler_params=pltpu.CompilerParams(vmem_limit_bytes=56 * 2**20, collective_id=0, has_side_effects=True),
        cost_estimate=pl.CostEstimate(flops=10**10, bytes_accessed=3 * 10**7, transcendentals=0),
        name="gather_gram",
    )(own, prev)


def exchange_kernel(layers, s, blocks, chi_h, clo_h, phi_h, plo_h, out, rows_o,
                    chi, clo, phi, plo, arr, yh, yl, xb, rl, rb, ss, sr, bs, br, rs, rr, csem, psem, rsem):
    dp = lax.axis_index("dp")
    f = lax.axis_index("factor")
    nf = lax.axis_size("factor")
    nb = chi.shape[0] // W
    to = [lax.rem(f + nf - layers * (2 * t + 1), nf) for t in range(2)]
    frm = [lax.rem(f + layers * (2 * t + 1), nf) for t in range(2)]
    barrier = pltpu.get_barrier_semaphore()
    for t in range(2):
        for off in range(8):
            pl.semaphore_signal(barrier, inc=1, device_id=(lax.rem(dp + off, 8), frm[t]), device_id_type=MESH)
            pl.semaphore_signal(barrier, inc=1, device_id=(lax.rem(dp + off, 8), to[t]), device_id_type=MESH)
    pl.semaphore_signal(barrier, inc=1, device_id=(dp, lax.rem(f + nf // 2, nf)), device_id_type=MESH)
    pl.semaphore_wait(barrier, 33)

    H = W // 2

    def part(g, off, t):
        peer = lax.rem(dp + off, 8)
        r = pl.ds(g * H, H)
        return pltpu.make_async_remote_copy(
            src_ref=s.at[peer, t, r], dst_ref=arr.at[dp, t, r], send_sem=ss.at[g, off, t], recv_sem=sr.at[g, dp, t],
            device_id=(peer, to[t]), device_id_type=MESH)

    sends = [[part(g, off, t) for off in range(8) for t in range(2)] for g in range(2)]
    for x in sends[0]:
        x.start()
    lp = [pltpu.make_async_copy(phi_h, phi, psem.at[0]), pltpu.make_async_copy(plo_h, plo, psem.at[1])]
    lc = {}
    for k in range(1, nb):
        a, b = slice(k * W, (k + 1) * W), slice(0, k * W)
        lc[k] = [pltpu.make_async_copy(chi_h.at[a, b], chi.at[a, b], csem.at[k, 0]),
                 pltpu.make_async_copy(clo_h.at[a, b], clo.at[a, b], csem.at[k, 1])]
    for k in range(1, nb):
        for x in lc[k]:
            x.start()
    for x in lp:
        x.start()
    lr = []
    for j in range(nb):
        idx = jnp.maximum(dp, j) * nb + jnp.minimum(dp, j)
        x = pltpu.make_async_copy(blocks.at[idx], rb.at[j], rsem.at[j])
        x.start()
        lr.append(x)
    for j in range(nb):
        lr[j].wait()
        v = rb[j]
        low = jnp.full((W, W), dp, jnp.int32) >= j
        rows_o[:, j * W:(j + 1) * W] = jnp.where(low, v, v.T)

    for x in sends[0]:
        x.wait_send()
    for x in sends[1]:
        x.start()
    edge = lax.rem(f // layers, 4) == 3

    def home(g, k, t, to_f):
        return pltpu.make_async_remote_copy(
            src_ref=xb.at[g, k, t], dst_ref=out.at[t, pl.ds(k * W, W), pl.ds(g * H, H)],
            send_sem=bs.at[g, k, t], recv_sem=br.at[g, k, t], device_id=(dp, to_f), device_id_type=MESH)

    def hop(g, k):
        return pltpu.make_async_remote_copy(
            src_ref=xb.at[g, k, 0], dst_ref=rl.at[g, k], send_sem=bs.at[g, k, 0], recv_sem=rr.at[g, k],
            device_id=(dp, lax.rem(f + nf // 2, nf)), device_id_type=MESH)

    def onward(g, k):
        return pltpu.make_async_remote_copy(
            src_ref=rl.at[g, k], dst_ref=out.at[0, pl.ds(k * W, W), pl.ds(g * H, H)],
            send_sem=rs.at[g, k], recv_sem=br.at[g, k, 0],
            device_id=(dp, lax.rem(f + layers + nf // 2, nf)), device_id_type=MESH)

    def relay(g, k):
        @pl.when(edge)
        def _():
            hop(g, k).wait_recv()
            onward(g, k).start()

    order = []
    for g in range(2):
        r = slice(g * H, (g + 1) * H)
        for k in range(nb):
            for t in range(2):
                pltpu.make_async_remote_copy(
                    src_ref=s.at[k, t, r], dst_ref=arr.at[k, t, r], send_sem=ss.at[g, 0, t], recv_sem=sr.at[g, k, t],
                    device_id=(dp, to[t]), device_id_type=MESH).wait_recv()
            y = jnp.concatenate([arr[k, 0, r], arr[k, 1, r]], axis=0).astype(f32)
            if k:
                if g == 0:
                    for x in lc[k]:
                        x.wait()
                b = slice(0, k * W)
                c = slice(k * W, (k + 1) * W)
                y = y - dot3((yh[g, :, b], yl[g, :, b]), (chi[c, b], clo[c, b]), NT)
            y = split(y)
            yh[g, :, k * W:(k + 1) * W] = y[0]
            yl[g, :, k * W:(k + 1) * W] = y[1]
        if g == 0:
            for x in lp:
                x.wait()
        for k in reversed(range(nb)):
            sl = slice(k * W, (k + 1) * W)
            zk = dot3((yh[g, :, sl], yl[g, :, sl]), (phi[k], plo[k]), NN)
            if k + 1 < nb:
                b = slice((k + 1) * W, nb * W)
                zk = zk - dot3((yh[g, :, b], yl[g, :, b]), (chi[b, sl], clo[b, sl]), NN)
            x = split(zk)
            yh[g, :, sl] = x[0]
            yl[g, :, sl] = x[1]
            for t in range(2):
                xb[g, k, t] = zk[t * H:(t + 1) * H].T.astype(bf)
            home(g, k, 1, frm[1]).start()

            @pl.when(edge)
            def _():
                hop(g, k).start()

            @pl.when(jnp.logical_not(edge))
            def _():
                home(g, k, 0, frm[0]).start()

            order.append((g, k))
            if len(order) > 1:
                relay(*order[-2])
    relay(*order[-1])
    for x in sends[1]:
        x.wait_send()
    for g, k in order:
        for t in range(2):
            home(g, k, t, frm[t]).wait()

        @pl.when(edge)
        def _():
            onward(g, k).wait_send()


def exchange_call(s, blocks, chi, clo, phi, plo, layers):
    n = chi.shape[0]
    nb = n // W
    an = pl.BlockSpec(memory_space=pl.ANY)
    vm = pl.BlockSpec(memory_space=pltpu.VMEM)
    D = pltpu.SemaphoreType.DMA
    V = pltpu.VMEM
    return pl.pallas_call(
        functools.partial(exchange_kernel, layers),
        out_shape=(jax.ShapeDtypeStruct((2, n, W), bf), jax.ShapeDtypeStruct((W, n), f32)),
        in_specs=[vm] + [an] * 5, out_specs=(an, vm),
        scratch_shapes=[V((n, n), bf), V((n, n), bf), V((nb, W, W), bf), V((nb, W, W), bf), V((nb, 2, W, W), bf),
                        V((2, W, n), bf), V((2, W, n), bf), V((2, nb, 2, W, W // 2), bf), V((2, nb, W, W // 2), bf), V((nb, W, W), f32),
                        D((2, 8, 2)), D((2, 8, 2)), D((2, nb, 2)), D((2, nb, 2)), D((2, nb)), D((2, nb)), D((nb, 2)), D((2,)), D((nb,))],
        compiler_params=pltpu.CompilerParams(vmem_limit_bytes=56 * 2**20, collective_id=1, has_side_effects=True),
        cost_estimate=pl.CostEstimate(flops=13 * 10**9, bytes_accessed=3 * 10**7, transcendentals=0),
        name="exchange_solve",
    )(s, blocks, chi, clo, phi, plo)


def per_device(features, previous, gradient):
    layers = lax.axis_size("factor") // 8
    shards = lax.axis_size("dp")
    block_size = previous.shape[1]
    weight = (1.0 - decay_rate) / (features.shape[0] * shards)
    blocks, shift = gather_call(features[:, 0, :].T, previous, layers, weight)
    tile_rows = gradient.shape[2]
    flat = gradient[0].reshape(2 * tile_rows, block_size)
    chi, clo, phi, plo, section_one = factor_call(blocks, flat, shift)
    result, own_rows = exchange_call(section_one, blocks, chi, clo, phi, plo, layers)
    return (own_rows[None], result[None])


def solution(mesh):
    placed = (P("dp", "factor", None), P("factor", None, None), P("factor", None, "dp", None))
    return jax.shard_map(
        per_device,
        mesh=mesh,
        in_specs=placed,
        out_specs=(P("factor", "dp", None), P("factor", None, None, "dp")),
        check_vma=False,
    )
```

```python
import math
import jax, jax.numpy as jnp, numpy as np, functools
from jax import lax
from jax.experimental import pallas as pl
from jax.experimental.pallas import tpu as pltpu
W=256

def inv2(a,b,c):
    r = 1.0/(a*c-b*b)
    return c*r, -b*r, a*r

def inv4(p):
    a,b,c = inv2(p[0][0],p[0][1],p[1][1])
    b00,b01,b10,b11 = p[0][2],p[0][3],p[1][2],p[1][3]
    w00=a*b00+b*b10; w01=a*b01+b*b11; w10=b*b00+c*b10; w11=b*b01+c*b11
    s00=p[2][2]-(b00*w00+b10*w10); s01=p[2][3]-(b00*w01+b10*w11); s11=p[3][3]-(b01*w01+b11*w11)
    d00,d01,d11=inv2(s00,s01,s11)
    x00=-(w00*d00+w01*d01); x01=-(w00*d01+w01*d11); x10=-(w10*d00+w11*d01); x11=-(w10*d01+w11*d11)
    t00=a-(x00*w00+x01*w01); t01=b-(x00*w10+x01*w11); t11=c-(x10*w10+x11*w11)
    return [[t00,t01,x00,x01],[t01,t11,x10,x11],[x00,x10,d00,d01],[x01,x11,d01,d11]]

def invq(p,q):
    if q==1: return [[1.0/p[0][0]]]
    if q==2:
        a,b,c=inv2(p[0][0],p[0][1],p[1][1]); return [[a,b],[b,c]]
    return inv4(p)

NN=(((1,),(0,)),((),())); NT=(((1,),(1,)),((),()))
bf=jnp.bfloat16; f32=jnp.float32
def split(x):
    hi=x.astype(bf); return hi,(x-hi.astype(f32)).astype(bf)
def dot3(a,b,dims):
    d=lambda x,y: lax.dot_general(x,y,dims,preferred_element_type=f32)
    return d(a[0],b[0])+(d(a[0],b[1])+d(a[1],b[0]))

def sweep(A, slot, q=4, n=128):
    lane = lax.broadcasted_iota(jnp.int32,(1,n),1)
    for s in range(0,n,q):
        rows=[A[s+i:s+i+1,:] for i in range(q)]
        p=[[jnp.broadcast_to(rows[i][:,s+j:s+j+1],(1,n)) if j>=i else None for j in range(q)] for i in range(q)]
        X=invq(p,q)
        inl=(lane>=s)&(lane<s+q)
        rm=[jnp.where(lane==s+i,1.0,jnp.where(inl,0.0,rows[i])) for i in range(q)]
        nr=[]
        for i in range(q):
            t=X[i][0]*rm[0]
            for j in range(1,q): t=t+X[i][j]*rm[j]
            nr.append(t)
        tiles=[]
        for r in range(0,n,8):
            T=A[r:r+8,:]
            cols=[jnp.broadcast_to(T[:,s+i:s+i+1],(8,n)) for i in range(q)]
            T=jnp.where(inl,0.0,T)
            if r<=s<r+8:
                ri=lax.broadcasted_iota(jnp.int32,(8,1),0)+r
                inr=(ri>=s)&(ri<s+q)
                T=jnp.where(inr,0.0,T)
                cols=[jnp.where(ri==s+i,-1.0,jnp.where(inr,0.0,cols[i])) for i in range(q)]
            for i in range(q): T=T-cols[i]*nr[i]
            tiles.append(T)
        A=jnp.concatenate(tiles,axis=0)
        slot(s//q)
    return A

def tables(nb, extra, slots):
    dst=np.zeros((nb,slots),np.int32); li=np.zeros((nb,slots),np.int32); rj=np.zeros((nb,slots),np.int32)
    dst[:]=nb-1
    for k in range(1,nb):
        t=0
        for j in range(k,nb):
            for i in range(j,nb+extra):
                if (i,j)==(k,k): continue
                dst[k,t]=i*nb+j; li[k,t]=i; rj[k,t]=j; t+=1
        assert t<=slots
    return dst,li,rj

def factor_kernel(nb, extra, interleave, dst_t, li_t, rj_t, a_hbm, g_hbm, shift, chi_hbm, clo_hbm, phi_o, plo_o, s_o,
                  blk, gst, chi, clo, uh, ul, ch, cl, half, asem, gsem, osem):
    nr=nb+extra
    cslots=nr-2
    first=[]; rest=[]
    for j in range(nb):
        for i in range(j,nb):
            c=pltpu.make_async_copy(a_hbm.at[i*nb+j], blk.at[i*nb+j], asem.at[i,j])
            (first if (i,j)==(0,0) else rest).append(c)
    rest.append(pltpu.make_async_copy(g_hbm, gst, gsem.at[0]))
    for c in first+rest: c.start()
    for c in first: c.wait()
    eye=jnp.where(lax.broadcasted_iota(jnp.int32,(128,128),0)==lax.broadcasted_iota(jnp.int32,(128,128),1),shift[0:1,0:1],0.0)

    def tile(k,t):
        d=dst_t[k,t]; i=li_t[k,t]; j=rj_t[k,t]
        blk[d]=blk[d]-dot3((ch[i],cl[i]),(uh[j],ul[j]),NT)

    def panel(i,k):
        u=split(blk[i*nb+k])
        uh[i]=u[0]; ul[i]=u[1]
        c=split(dot3(u,(phi_o[k],plo_o[k]),NN))
        ch[i]=c[0]; cl[i]=c[1]
        r=pl.ds(pl.multiple_of(i*W,W),W); cc=pl.ds(pl.multiple_of(k*W,W),W)
        chi[r,cc]=c[0]; clo[r,cc]=c[1]

    def step(k,_):
        kk=k*nb+k
        kp=jnp.maximum(k-1,0)
        def slot(h,s):
            if not interleave: return
            if h==0 and s<cslots: panel(jnp.minimum(k+1+s,nr-1),kp)
            else: tile(k,h*32+s-cslots)
        p1=sweep(blk[kk,:128,:128]+eye,lambda s: slot(0,s))
        half[0]=p1
        @pl.when(k==0)
        def _():
            for c in rest: c.wait()
            for j in range(nb):
                for e in range(extra):
                    blk[(nb+e)*nb+j]=gst[e*W:(e+1)*W,j*W:(j+1)*W].astype(f32)
        d21=split(blk[kk,128:,:128])
        w=dot3(d21,split(half[0]),NN)
        sw=split(w)
        half[2]=w
        p2v=sweep((blk[kk,128:,128:]+eye)-dot3(sw,d21,NT),lambda s: slot(1,s))
        p2=split(p2v); w=half[2]
        x21=-dot3(p2,split(w),NN)
        x11=half[0]-dot3(split(w.T),split(x21),NN)
        top=jnp.concatenate([x11,x21.T],axis=1)
        bot=jnp.concatenate([x21,p2v],axis=1)
        P=split(jnp.concatenate([top,bot],axis=0))
        phi_o[k]=P[0]; plo_o[k]=P[1]
        if not interleave:
            def lp(t,_):
                tile(k,t); return 0
            lax.fori_loop(0,jnp.where(k==0,0,jnp.int32(64)),lp,0)
            def lc(i,_):
                panel(i,k); return 0
            lax.fori_loop(k+2,nr,lc,0)
        panel(k+1,k)
        @pl.when(k+1<nb)
        def _():
            d=(k+1)*nb+k+1
            blk[d]=blk[d]-dot3((ch[k+1],cl[k+1]),(uh[k+1],ul[k+1]),NT)
        return 0
    lax.fori_loop(0,nb,step,0)
    o1=pltpu.make_async_copy(chi.at[pl.ds(0,nb*W)],chi_hbm,osem.at[0]); o2=pltpu.make_async_copy(clo.at[pl.ds(0,nb*W)],clo_hbm,osem.at[1])
    o1.start(); o2.start()
    for i in range(nb+1,nr): panel(i,nb-1)
    er=slice(nb*W,nr*W)
    for k in reversed(range(nb)):
        sl=slice(k*W,(k+1)*W)
        z=chi[er,sl].astype(f32)+clo[er,sl].astype(f32)
        if k+1<nb:
            b=slice((k+1)*W,nb*W)
            z=z-dot3((chi[er,b],clo[er,b]),(chi[b,sl],clo[b,sl]),NN)
        x=split(z)
        chi[er,sl]=x[0]; clo[er,sl]=x[1]
        for e in range(extra): s_o[k,e]=z[e*W:(e+1)*W].T.astype(bf)
    o1.wait(); o2.wait()
def factor_call(a,g,shift,interleave=True):
    n=g.shape[1]; nb=n//W; extra=g.shape[0]//W
    t=tables(nb,extra,64-(nb+extra-2))
    sm=pl.BlockSpec(memory_space=pltpu.SMEM); an=pl.BlockSpec(memory_space=pl.ANY); vm=pl.BlockSpec(memory_space=pltpu.VMEM)
    return pl.pallas_call(
        functools.partial(factor_kernel,nb,extra,interleave),
        out_shape=(jax.ShapeDtypeStruct((n,n),bf),jax.ShapeDtypeStruct((n,n),bf),jax.ShapeDtypeStruct((nb,W,W),bf),jax.ShapeDtypeStruct((nb,W,W),bf),jax.ShapeDtypeStruct((nb,extra,W,W),bf)),
        in_specs=[sm,sm,sm,an,an,vm], out_specs=(an,an,vm,vm,vm),
        scratch_shapes=[pltpu.VMEM(((nb+extra)*nb,W,W),f32),pltpu.VMEM((extra*W,n),bf),pltpu.VMEM((n+extra*W,n),bf),pltpu.VMEM((n+extra*W,n),bf),
            pltpu.VMEM((nb+extra,W,W),bf),pltpu.VMEM((nb+extra,W,W),bf),pltpu.VMEM((nb+extra,W,W),bf),pltpu.VMEM((nb+extra,W,W),bf),
            pltpu.VMEM((3,128,128),f32),pltpu.SemaphoreType.DMA((nb,nb)),pltpu.SemaphoreType.DMA((1,)),pltpu.SemaphoreType.DMA((2,))],
        compiler_params=pltpu.CompilerParams(vmem_limit_bytes=60*2**20),
        name="factor",
    )(*[jnp.asarray(x) for x in t],a,g,shift)


from jax.sharding import PartitionSpec as P

decay_rate = 0.5
damping = 0.1

MESH = pl.DeviceIdType.MESH


def gather_kernel(dec, weight, damp, layers, own, prev, blocks, c_o, ft, acc, diag, part, tr1, tr2, zs, zr, t1s, t1r, t2s, t2r, psem, osem, lsem):
    dp = lax.axis_index("dp")
    f = lax.axis_index("factor")
    nb = 8
    z, y = dp // 4, dp % 4
    oz = 1 - z
    up, down = z * 4 + (y + 1) % 4, z * 4 + (y + 3) % 4
    member, layer = f // layers, f % layers
    far = z * 4 + (y + 2) % 4
    other, oup, odown, ofar = oz * 4 + y, oz * 4 + (y + 1) % 4, oz * 4 + (y + 3) % 4, oz * 4 + (y + 2) % 4

    loads = {}
    for i in range(nb):
        for j in range(i + 1):
            loads[i, j] = pltpu.make_async_copy(
                prev.at[0, pl.ds(i * W, W), pl.ds(j * W, W)], acc.at[i * nb + j], psem.at[i, j])
    row = pl.ds(pl.multiple_of(dp * W, W), W)
    dcopy = pltpu.make_async_copy(prev.at[0, row, row], diag, lsem.at[0])
    mine = pltpu.make_async_copy(own, ft.at[dp], lsem.at[1])
    dcopy.start()
    mine.start()

    barrier = pltpu.get_barrier_semaphore()
    for off in range(1, 8):
        pl.semaphore_signal(barrier, inc=1, device_id=((dp + off) % 8, f), device_id_type=MESH)
        pl.semaphore_signal(barrier, inc=1, device_id=(dp, ((member + off) % 8) * layers + layer), device_id_type=MESH)
    pl.semaphore_wait(barrier, 14)

    CH = zs.shape[0]
    rows = ft.shape[1] // CH
    half = rows // 2

    def send(kind, c, src, slot, to, lo, n):
        r = pl.ds(c * rows + lo, n)
        return pltpu.make_async_remote_copy(
            src_ref=src.at[r], dst_ref=ft.at[slot, r], send_sem=zs.at[c, kind], recv_sem=zr.at[c, kind],
            device_id=(to, f), device_id_type=MESH)

    cp = {}
    for c in range(CH):
        cp[0, c] = send(0, c, own, dp, other, 0, rows)
        cp[1, c] = send(1, c, own, dp, up, 0, rows)
        cp[2, c] = send(2, c, own, dp, down, 0, rows)
        cp[3, c] = send(3, c, ft.at[down], down, up, 0, half)
        cp[4, c] = send(4, c, ft.at[up], up, down, half, half)
        cp[5, c] = send(5, c, ft.at[other], other, up, 0, half)
        cp[6, c] = send(6, c, ft.at[other], other, down, half, half)
        cp[7, c] = send(7, c, ft.at[odown], odown, up, 0, half)
        cp[8, c] = send(8, c, ft.at[oup], oup, down, half, half)
        cp[9, c] = send(9, c, ft.at[down], down, other, half, half)
        cp[10, c] = send(10, c, ft.at[up], up, other, 0, half)
    for c in range(CH):
        for kind in range(3):
            cp[kind, c].start()

    dcopy.wait()
    ii = lax.broadcasted_iota(jnp.int32, (W, W), 0)
    jj = lax.broadcasted_iota(jnp.int32, (W, W), 1)
    tr = jnp.sum(jnp.where(ii == jj, diag[...], 0.0))
    xs = own[...].astype(f32)
    share = dec * tr + weight * jnp.sum(xs * xs)
    part[0] = jnp.full((8, 128), share, f32)
    tr1[dp] = part[0]
    c1 = [pltpu.make_async_remote_copy(
        src_ref=part.at[0], dst_ref=tr1.at[dp], send_sem=t1s.at[off], recv_sem=t1r.at[off],
        device_id=((dp + off) % 8, f), device_id_type=MESH) for off in range(1, 8)]
    for x in c1:
        x.start()
    for x in loads.values():
        x.start()
    for x in c1:
        x.wait()
    total = tr1[0]
    for i in range(1, 8):
        total = total + tr1[i]
    part[1] = total
    tr2[member] = total
    c2 = [pltpu.make_async_remote_copy(
        src_ref=part.at[1], dst_ref=tr2.at[member], send_sem=t2s.at[off], recv_sem=t2r.at[off],
        device_id=(dp, ((member + off) % 8) * layers + layer), device_id_type=MESH) for off in range(1, 8)]
    for x in c2:
        x.start()

    per = nb // CH

    def tiles(c, slots, first):
        for i in range(c * per, (c + 1) * per):
            def body(j, _):
                d = None
                for s in slots:
                    t = lax.dot_general(ft[s, i * W:(i + 1) * W, :], ft[s, pl.ds(pl.multiple_of(j * W, W), W), :], NT, preferred_element_type=f32)
                    d = t if d is None else d + t
                old = acc[i * nb + j]
                acc[i * nb + j] = (dec * old if first else old) + weight * d
                return 0
            lax.fori_loop(0, i + 1, body, 0)

    for c in range(CH):
        cp[1, c].wait_recv()
        cp[3, c].start()
        cp[9, c].start()
        cp[2, c].wait_recv()
        cp[4, c].start()
        cp[10, c].start()
        cp[0, c].wait_recv()
        cp[5, c].start()
        cp[6, c].start()
    for x in loads.values():
        x.wait()
    mine.wait()
    for c in range(CH):
        tiles(c, [dp, down, up, other], True)
    for x in c2:
        x.wait()
    s_in = tr2[0] + tr2[2] + tr2[4] + tr2[6]
    s_out = tr2[1] + tr2[3] + tr2[5] + tr2[7]
    ratio = jnp.sqrt(s_in / s_out)
    even = (jnp.full((8, 128), member, jnp.int32) % 2) == 0
    c_o[...] = jnp.where(even, ratio, 1.0 / ratio) * damp
    for c in range(CH):
        cp[5, c].wait_recv()
        cp[7, c].start()
        cp[6, c].wait_recv()
        cp[8, c].start()
    for c in range(CH):
        for kind in (3, 4, 9, 10):
            cp[kind, c].wait_recv()
        tiles(c, [odown, oup, far], False)
    outs = []
    for c in range(CH):
        cp[7, c].wait_recv()
        cp[8, c].wait_recv()
        tiles(c, [ofar], False)
        for i in range(c * per, (c + 1) * per):
            for j in range(i + 1):
                o = pltpu.make_async_copy(acc.at[i * nb + j], blocks.at[i * nb + j], osem.at[i, j])
                o.start()
                outs.append(o)
    for x in cp.values():
        x.wait_send()
    for o in outs:
        o.wait()


def gather_call(own, prev, layers, weight):
    n, w = own.shape
    nb = n // W
    CH = 4
    an = pl.BlockSpec(memory_space=pl.ANY)
    vm = pl.BlockSpec(memory_space=pltpu.VMEM)
    D = pltpu.SemaphoreType.DMA
    return pl.pallas_call(
        functools.partial(gather_kernel, decay_rate, weight, math.sqrt(damping), layers),
        out_shape=(jax.ShapeDtypeStruct((nb * nb, W, W), f32), jax.ShapeDtypeStruct((8, 128), f32)),
        in_specs=[vm, an], out_specs=(an, vm),
        scratch_shapes=[pltpu.VMEM((8, n, w), bf), pltpu.VMEM((nb * nb, W, W), f32), pltpu.VMEM((W, W), f32),
                        pltpu.VMEM((2, 8, 128), f32), pltpu.VMEM((8, 8, 128), f32), pltpu.VMEM((8, 8, 128), f32),
                        D((CH, 11)), D((CH, 11)), D((8,)), D((8,)), D((8,)), D((8,)), D((nb, nb)), D((nb, nb)), D((2,))],
        compiler_params=pltpu.CompilerParams(vmem_limit_bytes=56 * 2**20, collective_id=0, has_side_effects=True),
        cost_estimate=pl.CostEstimate(flops=10**10, bytes_accessed=3 * 10**7, transcendentals=0),
        name="gather_gram",
    )(own, prev)


def exchange_kernel(layers, s, blocks, chi_h, clo_h, phi_h, plo_h, out, rows_o,
                    chi, clo, phi, plo, arr, yh, yl, xb, rl, rb, ss, sr, bs, br, rs, rr, csem, psem, rsem):
    dp = lax.axis_index("dp")
    f = lax.axis_index("factor")
    nf = lax.axis_size("factor")
    nb = chi.shape[0] // W
    to = [lax.rem(f + nf - layers * (2 * t + 1), nf) for t in range(2)]
    frm = [lax.rem(f + layers * (2 * t + 1), nf) for t in range(2)]
    barrier = pltpu.get_barrier_semaphore()
    for t in range(2):
        for off in range(8):
            pl.semaphore_signal(barrier, inc=1, device_id=(lax.rem(dp + off, 8), frm[t]), device_id_type=MESH)
            pl.semaphore_signal(barrier, inc=1, device_id=(lax.rem(dp + off, 8), to[t]), device_id_type=MESH)
    pl.semaphore_signal(barrier, inc=1, device_id=(dp, lax.rem(f + nf // 2, nf)), device_id_type=MESH)
    pl.semaphore_wait(barrier, 33)

    H = W // 2

    def part(g, off, t):
        peer = lax.rem(dp + off, 8)
        r = pl.ds(g * H, H)
        return pltpu.make_async_remote_copy(
            src_ref=s.at[peer, t, r], dst_ref=arr.at[dp, t, r], send_sem=ss.at[g, off, t], recv_sem=sr.at[g, dp, t],
            device_id=(peer, to[t]), device_id_type=MESH)

    sends = [[part(g, off, t) for off in range(8) for t in range(2)] for g in range(2)]
    for x in sends[0]:
        x.start()
    lp = [pltpu.make_async_copy(phi_h, phi, psem.at[0]), pltpu.make_async_copy(plo_h, plo, psem.at[1])]
    lc = {}
    for k in range(1, nb):
        a, b = slice(k * W, (k + 1) * W), slice(0, k * W)
        lc[k] = [pltpu.make_async_copy(chi_h.at[a, b], chi.at[a, b], csem.at[k, 0]),
                 pltpu.make_async_copy(clo_h.at[a, b], clo.at[a, b], csem.at[k, 1])]
    for k in range(1, nb):
        for x in lc[k]:
            x.start()
    for x in lp:
        x.start()
    lr = []
    for j in range(nb):
        idx = jnp.maximum(dp, j) * nb + jnp.minimum(dp, j)
        x = pltpu.make_async_copy(blocks.at[idx], rb.at[j], rsem.at[j])
        x.start()
        lr.append(x)
    for j in range(nb):
        lr[j].wait()
        v = rb[j]
        low = jnp.full((W, W), dp, jnp.int32) >= j
        rows_o[:, j * W:(j + 1) * W] = jnp.where(low, v, v.T)

    for x in sends[0]:
        x.wait_send()
    for x in sends[1]:
        x.start()
    edge = lax.rem(f // layers, 4) == 3

    def home(g, k, t, to_f):
        return pltpu.make_async_remote_copy(
            src_ref=xb.at[g, k, t], dst_ref=out.at[t, pl.ds(k * W, W), pl.ds(g * H, H)],
            send_sem=bs.at[g, k, t], recv_sem=br.at[g, k, t], device_id=(dp, to_f), device_id_type=MESH)

    def hop(g, k):
        return pltpu.make_async_remote_copy(
            src_ref=xb.at[g, k, 0], dst_ref=rl.at[g, k], send_sem=bs.at[g, k, 0], recv_sem=rr.at[g, k],
            device_id=(dp, lax.rem(f + nf // 2, nf)), device_id_type=MESH)

    def onward(g, k):
        return pltpu.make_async_remote_copy(
            src_ref=rl.at[g, k], dst_ref=out.at[0, pl.ds(k * W, W), pl.ds(g * H, H)],
            send_sem=rs.at[g, k], recv_sem=br.at[g, k, 0],
            device_id=(dp, lax.rem(f + layers + nf // 2, nf)), device_id_type=MESH)

    def relay(g, k):
        @pl.when(edge)
        def _():
            hop(g, k).wait_recv()
            onward(g, k).start()

    order = []
    for g in range(2):
        r = slice(g * H, (g + 1) * H)
        for k in range(nb):
            for t in range(2):
                pltpu.make_async_remote_copy(
                    src_ref=s.at[k, t, r], dst_ref=arr.at[k, t, r], send_sem=ss.at[g, 0, t], recv_sem=sr.at[g, k, t],
                    device_id=(dp, to[t]), device_id_type=MESH).wait_recv()
            y = jnp.concatenate([arr[k, 0, r], arr[k, 1, r]], axis=0).astype(f32)
            if k:
                if g == 0:
                    for x in lc[k]:
                        x.wait()
                b = slice(0, k * W)
                c = slice(k * W, (k + 1) * W)
                y = y - dot3((yh[g, :, b], yl[g, :, b]), (chi[c, b], clo[c, b]), NT)
            if g == 1:
                relay(0, nb - 1 - k)
            y = split(y)
            yh[g, :, k * W:(k + 1) * W] = y[0]
            yl[g, :, k * W:(k + 1) * W] = y[1]
        if g == 0:
            for x in lp:
                x.wait()
        for k in reversed(range(nb)):
            sl = slice(k * W, (k + 1) * W)
            zk = dot3((yh[g, :, sl], yl[g, :, sl]), (phi[k], plo[k]), NN)
            if k + 1 < nb:
                b = slice((k + 1) * W, nb * W)
                zk = zk - dot3((yh[g, :, b], yl[g, :, b]), (chi[b, sl], clo[b, sl]), NN)
            x = split(zk)
            yh[g, :, sl] = x[0]
            yl[g, :, sl] = x[1]
            for t in range(2):
                xb[g, k, t] = zk[t * H:(t + 1) * H].T.astype(bf)
            home(g, k, 1, frm[1]).start()

            @pl.when(edge)
            def _():
                hop(g, k).start()

            @pl.when(jnp.logical_not(edge))
            def _():
                home(g, k, 0, frm[0]).start()

            order.append((g, k))
    for k in reversed(range(nb)):
        relay(1, k)
    for x in sends[1]:
        x.wait_send()
    for g, k in order:
        for t in range(2):
            home(g, k, t, frm[t]).wait()

        @pl.when(edge)
        def _():
            onward(g, k).wait_send()


def exchange_call(s, blocks, chi, clo, phi, plo, layers):
    n = chi.shape[0]
    nb = n // W
    an = pl.BlockSpec(memory_space=pl.ANY)
    vm = pl.BlockSpec(memory_space=pltpu.VMEM)
    D = pltpu.SemaphoreType.DMA
    V = pltpu.VMEM
    return pl.pallas_call(
        functools.partial(exchange_kernel, layers),
        out_shape=(jax.ShapeDtypeStruct((2, n, W), bf), jax.ShapeDtypeStruct((W, n), f32)),
        in_specs=[vm] + [an] * 5, out_specs=(an, vm),
        scratch_shapes=[V((n, n), bf), V((n, n), bf), V((nb, W, W), bf), V((nb, W, W), bf), V((nb, 2, W, W), bf),
                        V((2, W, n), bf), V((2, W, n), bf), V((2, nb, 2, W, W // 2), bf), V((2, nb, W, W // 2), bf), V((nb, W, W), f32),
                        D((2, 8, 2)), D((2, 8, 2)), D((2, nb, 2)), D((2, nb, 2)), D((2, nb)), D((2, nb)), D((nb, 2)), D((2,)), D((nb,))],
        compiler_params=pltpu.CompilerParams(vmem_limit_bytes=56 * 2**20, collective_id=1, has_side_effects=True),
        cost_estimate=pl.CostEstimate(flops=13 * 10**9, bytes_accessed=3 * 10**7, transcendentals=0),
        name="exchange_solve",
    )(s, blocks, chi, clo, phi, plo)


def per_device(features, previous, gradient):
    layers = lax.axis_size("factor") // 8
    shards = lax.axis_size("dp")
    block_size = previous.shape[1]
    weight = (1.0 - decay_rate) / (features.shape[0] * shards)
    blocks, shift = gather_call(features[:, 0, :].T, previous, layers, weight)
    tile_rows = gradient.shape[2]
    flat = gradient[0].reshape(2 * tile_rows, block_size)
    chi, clo, phi, plo, section_one = factor_call(blocks, flat, shift)
    result, own_rows = exchange_call(section_one, blocks, chi, clo, phi, plo, layers)
    return (own_rows[None], result[None])


def solution(mesh):
    placed = (P("dp", "factor", None), P("factor", None, None), P("factor", None, "dp", None))
    return jax.shard_map(
        per_device,
        mesh=mesh,
        in_specs=placed,
        out_specs=(P("factor", "dp", None), P("factor", None, None, "dp")),
        check_vma=False,
    )
```

```python
import math
import jax, jax.numpy as jnp, numpy as np, functools
from jax import lax
from jax.experimental import pallas as pl
from jax.experimental.pallas import tpu as pltpu
W=256

def inv2(a,b,c):
    r = 1.0/(a*c-b*b)
    return c*r, -b*r, a*r

def inv4(p):
    a,b,c = inv2(p[0][0],p[0][1],p[1][1])
    b00,b01,b10,b11 = p[0][2],p[0][3],p[1][2],p[1][3]
    w00=a*b00+b*b10; w01=a*b01+b*b11; w10=b*b00+c*b10; w11=b*b01+c*b11
    s00=p[2][2]-(b00*w00+b10*w10); s01=p[2][3]-(b00*w01+b10*w11); s11=p[3][3]-(b01*w01+b11*w11)
    d00,d01,d11=inv2(s00,s01,s11)
    x00=-(w00*d00+w01*d01); x01=-(w00*d01+w01*d11); x10=-(w10*d00+w11*d01); x11=-(w10*d01+w11*d11)
    t00=a-(x00*w00+x01*w01); t01=b-(x00*w10+x01*w11); t11=c-(x10*w10+x11*w11)
    return [[t00,t01,x00,x01],[t01,t11,x10,x11],[x00,x10,d00,d01],[x01,x11,d01,d11]]

def invq(p,q):
    if q==1: return [[1.0/p[0][0]]]
    if q==2:
        a,b,c=inv2(p[0][0],p[0][1],p[1][1]); return [[a,b],[b,c]]
    return inv4(p)

NN=(((1,),(0,)),((),())); NT=(((1,),(1,)),((),()))
bf=jnp.bfloat16; f32=jnp.float32
def split(x):
    hi=x.astype(bf); return hi,(x-hi.astype(f32)).astype(bf)
def dot3(a,b,dims):
    d=lambda x,y: lax.dot_general(x,y,dims,preferred_element_type=f32)
    return d(a[0],b[0])+(d(a[0],b[1])+d(a[1],b[0]))

def sweep(A, slot, q=4, n=128):
    lane = lax.broadcasted_iota(jnp.int32,(1,n),1)
    for s in range(0,n,q):
        rows=[A[s+i:s+i+1,:] for i in range(q)]
        p=[[jnp.broadcast_to(rows[i][:,s+j:s+j+1],(1,n)) if j>=i else None for j in range(q)] for i in range(q)]
        X=invq(p,q)
        inl=(lane>=s)&(lane<s+q)
        rm=[jnp.where(lane==s+i,1.0,jnp.where(inl,0.0,rows[i])) for i in range(q)]
        nr=[]
        for i in range(q):
            t=X[i][0]*rm[0]
            for j in range(1,q): t=t+X[i][j]*rm[j]
            nr.append(t)
        tiles=[]
        for r in range(0,n,8):
            T=A[r:r+8,:]
            cols=[jnp.broadcast_to(T[:,s+i:s+i+1],(8,n)) for i in range(q)]
            T=jnp.where(inl,0.0,T)
            if r<=s<r+8:
                ri=lax.broadcasted_iota(jnp.int32,(8,1),0)+r
                inr=(ri>=s)&(ri<s+q)
                T=jnp.where(inr,0.0,T)
                cols=[jnp.where(ri==s+i,-1.0,jnp.where(inr,0.0,cols[i])) for i in range(q)]
            for i in range(q): T=T-cols[i]*nr[i]
            tiles.append(T)
        A=jnp.concatenate(tiles,axis=0)
        slot(s//q)
    return A

def tables(nb, extra, slots):
    dst=np.zeros((nb,slots),np.int32); li=np.zeros((nb,slots),np.int32); rj=np.zeros((nb,slots),np.int32)
    dst[:]=nb-1
    for k in range(1,nb):
        t=0
        for j in range(k,nb):
            for i in range(j,nb+extra):
                if (i,j)==(k,k): continue
                dst[k,t]=i*nb+j; li[k,t]=i; rj[k,t]=j; t+=1
        assert t<=slots
    return dst,li,rj

def factor_kernel(nb, extra, sharded, dst_t, li_t, rj_t, a_hbm, g_hbm, shift, chi_hbm, clo_hbm, phi_o, plo_o, s_o, rows_o,
                  rows_v, blk, gst, chi, clo, uh, ul, ch, cl, half, asem, gsem, osem):
    nr=nb+extra
    cslots=nr-2
    first=[]; rest=[]
    for j in range(nb):
        for i in range(j,nb):
            c=pltpu.make_async_copy(a_hbm.at[i*nb+j], blk.at[i*nb+j], asem.at[i,j])
            (first if (i,j)==(0,0) else rest).append(c)
    rest.append(pltpu.make_async_copy(g_hbm, gst, gsem.at[0]))
    for c in first+rest: c.start()
    for c in first: c.wait()
    eye=jnp.where(lax.broadcasted_iota(jnp.int32,(128,128),0)==lax.broadcasted_iota(jnp.int32,(128,128),1),shift[0:1,0:1],0.0)

    def tile(k,t):
        d=dst_t[k,t]; i=li_t[k,t]; j=rj_t[k,t]
        blk[d]=blk[d]-dot3((ch[i],cl[i]),(uh[j],ul[j]),NT)

    orow=pltpu.make_async_copy(rows_v,rows_o,osem.at[2])
    def own_rows():
        dp=lax.axis_index("dp") if sharded else 3
        for j in range(nb):
            v=blk[jnp.maximum(dp,j)*nb+jnp.minimum(dp,j)]
            rows_v[:,j*W:(j+1)*W]=jnp.where(jnp.full((W,W),dp,jnp.int32)>=j,v,v.T)

    def panel(i,k):
        u=split(blk[i*nb+k])
        uh[i]=u[0]; ul[i]=u[1]
        c=split(dot3(u,(phi_o[k],plo_o[k]),NN))
        ch[i]=c[0]; cl[i]=c[1]
        r=pl.ds(pl.multiple_of(i*W,W),W); cc=pl.ds(pl.multiple_of(k*W,W),W)
        chi[r,cc]=c[0]; clo[r,cc]=c[1]

    def step(k,_):
        kk=k*nb+k
        kp=jnp.maximum(k-1,0)
        def slot(h,s):
            if h==0 and s<2*cslots:
                if s%2==0: panel(jnp.minimum(k+1+s//2,nr-1),kp)
            else: tile(k,h*32+s-2*cslots)
        p1=sweep(blk[kk,:128,:128]+eye,lambda s: slot(0,s))
        half[0]=p1
        @pl.when(k==0)
        def _():
            for c in rest: c.wait()
            for j in range(nb):
                for e in range(extra):
                    blk[(nb+e)*nb+j]=gst[e*W:(e+1)*W,j*W:(j+1)*W].astype(f32)
            own_rows()
        d21=split(blk[kk,128:,:128])
        w=dot3(d21,split(half[0]),NN)
        sw=split(w)
        half[2]=w
        p2v=sweep((blk[kk,128:,128:]+eye)-dot3(sw,d21,NT),lambda s: slot(1,s))
        p2=split(p2v); w=half[2]
        x21=-dot3(p2,split(w),NN)
        x11=half[0]-dot3(split(w.T),split(x21),NN)
        top=jnp.concatenate([x11,x21.T],axis=1)
        bot=jnp.concatenate([x21,p2v],axis=1)
        P=split(jnp.concatenate([top,bot],axis=0))
        phi_o[k]=P[0]; plo_o[k]=P[1]
        panel(k+1,k)
        @pl.when(k+1<nb)
        def _():
            d=(k+1)*nb+k+1
            blk[d]=blk[d]-dot3((ch[k+1],cl[k+1]),(uh[k+1],ul[k+1]),NT)
        return 0
    lax.fori_loop(0,nb,step,0)
    o1=pltpu.make_async_copy(chi.at[pl.ds(0,nb*W)],chi_hbm,osem.at[0]); o2=pltpu.make_async_copy(clo.at[pl.ds(0,nb*W)],clo_hbm,osem.at[1])
    o1.start(); o2.start()
    for i in range(nb+1,nr): panel(i,nb-1)
    orow.start()
    er=slice(nb*W,nr*W)
    for k in reversed(range(nb)):
        sl=slice(k*W,(k+1)*W)
        z=chi[er,sl].astype(f32)+clo[er,sl].astype(f32)
        if k+1<nb:
            b=slice((k+1)*W,nb*W)
            z=z-dot3((chi[er,b],clo[er,b]),(chi[b,sl],clo[b,sl]),NN)
        x=split(z)
        chi[er,sl]=x[0]; clo[er,sl]=x[1]
        for e in range(extra): s_o[k,e]=z[e*W:(e+1)*W].T.astype(bf)
    o1.wait(); o2.wait(); orow.wait()
def factor_call(a,g,shift,sharded=True):
    n=g.shape[1]; nb=n//W; extra=g.shape[0]//W
    t=tables(nb,extra,64-2*(nb+extra-2))
    sm=pl.BlockSpec(memory_space=pltpu.SMEM); an=pl.BlockSpec(memory_space=pl.ANY); vm=pl.BlockSpec(memory_space=pltpu.VMEM)
    return pl.pallas_call(
        functools.partial(factor_kernel,nb,extra,sharded),
        out_shape=(jax.ShapeDtypeStruct((n,n),bf),jax.ShapeDtypeStruct((n,n),bf),jax.ShapeDtypeStruct((nb,W,W),bf),jax.ShapeDtypeStruct((nb,W,W),bf),jax.ShapeDtypeStruct((nb,extra,W,W),bf),jax.ShapeDtypeStruct((W,n),f32)),
        in_specs=[sm,sm,sm,an,an,vm], out_specs=(an,an,vm,vm,vm,an),
        scratch_shapes=[pltpu.VMEM((W,n),f32),pltpu.VMEM(((nb+extra)*nb,W,W),f32),pltpu.VMEM((extra*W,n),bf),pltpu.VMEM((n+extra*W,n),bf),pltpu.VMEM((n+extra*W,n),bf),
            pltpu.VMEM((nb+extra,W,W),bf),pltpu.VMEM((nb+extra,W,W),bf),pltpu.VMEM((nb+extra,W,W),bf),pltpu.VMEM((nb+extra,W,W),bf),
            pltpu.VMEM((3,128,128),f32),pltpu.SemaphoreType.DMA((nb,nb)),pltpu.SemaphoreType.DMA((1,)),pltpu.SemaphoreType.DMA((3,))],
        compiler_params=pltpu.CompilerParams(vmem_limit_bytes=60*2**20),
        name="factor",
    )(*[jnp.asarray(x) for x in t],a,g,shift)


from jax.sharding import PartitionSpec as P

decay_rate = 0.5
damping = 0.1

MESH = pl.DeviceIdType.MESH


def gather_kernel(dec, weight, damp, layers, own, prev, blocks, c_o, ft, acc, diag, part, tr1, tr2, zs, zr, t1s, t1r, t2s, t2r, psem, osem, lsem):
    dp = lax.axis_index("dp")
    f = lax.axis_index("factor")
    nb = 8
    z, y = dp // 4, dp % 4
    oz = 1 - z
    up, down = z * 4 + (y + 1) % 4, z * 4 + (y + 3) % 4
    member, layer = f // layers, f % layers
    far = z * 4 + (y + 2) % 4
    other, oup, odown, ofar = oz * 4 + y, oz * 4 + (y + 1) % 4, oz * 4 + (y + 3) % 4, oz * 4 + (y + 2) % 4

    loads = {}
    for i in range(nb):
        for j in range(i + 1):
            loads[i, j] = pltpu.make_async_copy(
                prev.at[0, pl.ds(i * W, W), pl.ds(j * W, W)], acc.at[i * nb + j], psem.at[i, j])
    row = pl.ds(pl.multiple_of(dp * W, W), W)
    dcopy = pltpu.make_async_copy(prev.at[0, row, row], diag, lsem.at[0])
    mine = pltpu.make_async_copy(own, ft.at[dp], lsem.at[1])
    dcopy.start()
    mine.start()

    barrier = pltpu.get_barrier_semaphore()
    for off in range(1, 8):
        pl.semaphore_signal(barrier, inc=1, device_id=((dp + off) % 8, f), device_id_type=MESH)
        pl.semaphore_signal(barrier, inc=1, device_id=(dp, ((member + off) % 8) * layers + layer), device_id_type=MESH)
    pl.semaphore_wait(barrier, 14)

    CH = zs.shape[0]
    rows = ft.shape[1] // CH
    half = rows // 2

    def send(kind, c, src, slot, to, lo, n):
        r = pl.ds(c * rows + lo, n)
        return pltpu.make_async_remote_copy(
            src_ref=src.at[r], dst_ref=ft.at[slot, r], send_sem=zs.at[c, kind], recv_sem=zr.at[c, kind],
            device_id=(to, f), device_id_type=MESH)

    cp = {}
    for c in range(CH):
        cp[0, c] = send(0, c, own, dp, other, 0, rows)
        cp[1, c] = send(1, c, own, dp, up, 0, rows)
        cp[2, c] = send(2, c, own, dp, down, 0, rows)
        cp[3, c] = send(3, c, ft.at[down], down, up, 0, half)
        cp[4, c] = send(4, c, ft.at[up], up, down, half, half)
        cp[5, c] = send(5, c, ft.at[other], other, up, 0, half)
        cp[6, c] = send(6, c, ft.at[other], other, down, half, half)
        cp[7, c] = send(7, c, ft.at[odown], odown, up, 0, half)
        cp[8, c] = send(8, c, ft.at[oup], oup, down, half, half)
        cp[9, c] = send(9, c, ft.at[down], down, other, half, half)
        cp[10, c] = send(10, c, ft.at[up], up, other, 0, half)
    for c in range(CH):
        for kind in range(3):
            cp[kind, c].start()

    dcopy.wait()
    ii = lax.broadcasted_iota(jnp.int32, (W, W), 0)
    jj = lax.broadcasted_iota(jnp.int32, (W, W), 1)
    tr = jnp.sum(jnp.where(ii == jj, diag[...], 0.0))
    xs = own[...].astype(f32)
    share = dec * tr + weight * jnp.sum(xs * xs)
    part[0] = jnp.full((8, 128), share, f32)
    tr1[dp] = part[0]
    c1 = [pltpu.make_async_remote_copy(
        src_ref=part.at[0], dst_ref=tr1.at[dp], send_sem=t1s.at[off], recv_sem=t1r.at[off],
        device_id=((dp + off) % 8, f), device_id_type=MESH) for off in range(1, 8)]
    for x in c1:
        x.start()
    for x in loads.values():
        x.start()
    for x in c1:
        x.wait()
    total = tr1[0]
    for i in range(1, 8):
        total = total + tr1[i]
    part[1] = total
    tr2[member] = total
    c2 = [pltpu.make_async_remote_copy(
        src_ref=part.at[1], dst_ref=tr2.at[member], send_sem=t2s.at[off], recv_sem=t2r.at[off],
        device_id=(dp, ((member + off) % 8) * layers + layer), device_id_type=MESH) for off in range(1, 8)]
    for x in c2:
        x.start()

    per = nb // CH

    def tiles(c, slots, first):
        for i in range(c * per, (c + 1) * per):
            def body(j, _):
                d = None
                for s in slots:
                    t = lax.dot_general(ft[s, i * W:(i + 1) * W, :], ft[s, pl.ds(pl.multiple_of(j * W, W), W), :], NT, preferred_element_type=f32)
                    d = t if d is None else d + t
                old = acc[i * nb + j]
                acc[i * nb + j] = (dec * old if first else old) + weight * d
                return 0
            lax.fori_loop(0, i + 1, body, 0)

    for c in range(CH):
        cp[1, c].wait_recv()
        cp[3, c].start()
        cp[9, c].start()
        cp[2, c].wait_recv()
        cp[4, c].start()
        cp[10, c].start()
        cp[0, c].wait_recv()
        cp[5, c].start()
        cp[6, c].start()
    for x in loads.values():
        x.wait()
    mine.wait()
    for c in range(CH):
        tiles(c, [dp, down, up, other], True)
    for x in c2:
        x.wait()
    s_in = tr2[0] + tr2[2] + tr2[4] + tr2[6]
    s_out = tr2[1] + tr2[3] + tr2[5] + tr2[7]
    ratio = jnp.sqrt(s_in / s_out)
    even = (jnp.full((8, 128), member, jnp.int32) % 2) == 0
    c_o[...] = jnp.where(even, ratio, 1.0 / ratio) * damp
    for c in range(CH):
        cp[5, c].wait_recv()
        cp[7, c].start()
        cp[6, c].wait_recv()
        cp[8, c].start()
    for c in range(CH):
        for kind in (3, 4, 9, 10):
            cp[kind, c].wait_recv()
        tiles(c, [odown, oup, far], False)
    outs = []
    for c in range(CH):
        cp[7, c].wait_recv()
        cp[8, c].wait_recv()
        tiles(c, [ofar], False)
        for i in range(c * per, (c + 1) * per):
            for j in range(i + 1):
                o = pltpu.make_async_copy(acc.at[i * nb + j], blocks.at[i * nb + j], osem.at[i, j])
                o.start()
                outs.append(o)
    for x in cp.values():
        x.wait_send()
    for o in outs:
        o.wait()


def gather_call(own, prev, layers, weight):
    n, w = own.shape
    nb = n // W
    CH = 8
    an = pl.BlockSpec(memory_space=pl.ANY)
    vm = pl.BlockSpec(memory_space=pltpu.VMEM)
    D = pltpu.SemaphoreType.DMA
    return pl.pallas_call(
        functools.partial(gather_kernel, decay_rate, weight, math.sqrt(damping), layers),
        out_shape=(jax.ShapeDtypeStruct((nb * nb, W, W), f32), jax.ShapeDtypeStruct((8, 128), f32)),
        in_specs=[vm, an], out_specs=(an, vm),
        scratch_shapes=[pltpu.VMEM((8, n, w), bf), pltpu.VMEM((nb * nb, W, W), f32), pltpu.VMEM((W, W), f32),
                        pltpu.VMEM((2, 8, 128), f32), pltpu.VMEM((8, 8, 128), f32), pltpu.VMEM((8, 8, 128), f32),
                        D((CH, 11)), D((CH, 11)), D((8,)), D((8,)), D((8,)), D((8,)), D((nb, nb)), D((nb, nb)), D((2,))],
        compiler_params=pltpu.CompilerParams(vmem_limit_bytes=56 * 2**20, collective_id=0, has_side_effects=True),
        cost_estimate=pl.CostEstimate(flops=10**10, bytes_accessed=3 * 10**7, transcendentals=0),
        name="gather_gram",
    )(own, prev)


def exchange_kernel(layers, s, chi_h, clo_h, phi_h, plo_h, out,
                    chi, clo, phi, plo, arr, yh, yl, xb, rl, ss, sr, bs, br, rs, rr, csem, psem):
    dp = lax.axis_index("dp")
    f = lax.axis_index("factor")
    nf = lax.axis_size("factor")
    nb = chi.shape[0] // W
    to = [lax.rem(f + nf - layers * (2 * t + 1), nf) for t in range(2)]
    frm = [lax.rem(f + layers * (2 * t + 1), nf) for t in range(2)]
    barrier = pltpu.get_barrier_semaphore()
    for t in range(2):
        for off in range(8):
            pl.semaphore_signal(barrier, inc=1, device_id=(lax.rem(dp + off, 8), frm[t]), device_id_type=MESH)
            pl.semaphore_signal(barrier, inc=1, device_id=(lax.rem(dp + off, 8), to[t]), device_id_type=MESH)
    pl.semaphore_signal(barrier, inc=1, device_id=(dp, lax.rem(f + nf // 2, nf)), device_id_type=MESH)
    pl.semaphore_wait(barrier, 33)

    H = W // 2

    def part(g, off, t):
        peer = lax.rem(dp + off, 8)
        r = pl.ds(g * H, H)
        return pltpu.make_async_remote_copy(
            src_ref=s.at[peer, t, r], dst_ref=arr.at[dp, t, r], send_sem=ss.at[g, off, t], recv_sem=sr.at[g, dp, t],
            device_id=(peer, to[t]), device_id_type=MESH)

    sends = [[part(g, off, t) for off in range(8) for t in range(2)] for g in range(2)]
    for x in sends[0]:
        x.start()
    lp = [pltpu.make_async_copy(phi_h, phi, psem.at[0]), pltpu.make_async_copy(plo_h, plo, psem.at[1])]
    lc = {}
    for k in range(1, nb):
        a, b = slice(k * W, (k + 1) * W), slice(0, k * W)
        lc[k] = [pltpu.make_async_copy(chi_h.at[a, b], chi.at[a, b], csem.at[k, 0]),
                 pltpu.make_async_copy(clo_h.at[a, b], clo.at[a, b], csem.at[k, 1])]
    for k in range(1, nb):
        for x in lc[k]:
            x.start()
    for x in lp:
        x.start()
    for x in sends[0]:
        x.wait_send()
    for x in sends[1]:
        x.start()
    edge = lax.rem(f // layers, 4) == 3

    def home(g, k, t, to_f):
        return pltpu.make_async_remote_copy(
            src_ref=xb.at[g, k, t], dst_ref=out.at[t, pl.ds(k * W, W), pl.ds(g * H, H)],
            send_sem=bs.at[g, k, t], recv_sem=br.at[g, k, t], device_id=(dp, to_f), device_id_type=MESH)

    def hop(g, k):
        return pltpu.make_async_remote_copy(
            src_ref=xb.at[g, k, 0], dst_ref=rl.at[g, k], send_sem=bs.at[g, k, 0], recv_sem=rr.at[g, k],
            device_id=(dp, lax.rem(f + nf // 2, nf)), device_id_type=MESH)

    def onward(g, k):
        return pltpu.make_async_remote_copy(
            src_ref=rl.at[g, k], dst_ref=out.at[0, pl.ds(k * W, W), pl.ds(g * H, H)],
            send_sem=rs.at[g, k], recv_sem=br.at[g, k, 0],
            device_id=(dp, lax.rem(f + layers + nf // 2, nf)), device_id_type=MESH)

    def relay(g, k):
        @pl.when(edge)
        def _():
            hop(g, k).wait_recv()
            onward(g, k).start()

    order = []
    for g in range(2):
        r = slice(g * H, (g + 1) * H)
        for k in range(nb):
            for t in range(2):
                pltpu.make_async_remote_copy(
                    src_ref=s.at[k, t, r], dst_ref=arr.at[k, t, r], send_sem=ss.at[g, 0, t], recv_sem=sr.at[g, k, t],
                    device_id=(dp, to[t]), device_id_type=MESH).wait_recv()
            y = jnp.concatenate([arr[k, 0, r], arr[k, 1, r]], axis=0).astype(f32)
            if k:
                if g == 0:
                    for x in lc[k]:
                        x.wait()
                b = slice(0, k * W)
                c = slice(k * W, (k + 1) * W)
                y = y - dot3((yh[g, :, b], yl[g, :, b]), (chi[c, b], clo[c, b]), NT)
            if g == 1:
                relay(0, nb - 1 - k)
            y = split(y)
            yh[g, :, k * W:(k + 1) * W] = y[0]
            yl[g, :, k * W:(k + 1) * W] = y[1]
        if g == 0:
            for x in lp:
                x.wait()
        for k in reversed(range(nb)):
            sl = slice(k * W, (k + 1) * W)
            zk = dot3((yh[g, :, sl], yl[g, :, sl]), (phi[k], plo[k]), NN)
            if k + 1 < nb:
                b = slice((k + 1) * W, nb * W)
                zk = zk - dot3((yh[g, :, b], yl[g, :, b]), (chi[b, sl], clo[b, sl]), NN)
            x = split(zk)
            yh[g, :, sl] = x[0]
            yl[g, :, sl] = x[1]
            for t in range(2):
                xb[g, k, t] = zk[t * H:(t + 1) * H].T.astype(bf)
            home(g, k, 1, frm[1]).start()

            @pl.when(edge)
            def _():
                hop(g, k).start()

            @pl.when(jnp.logical_not(edge))
            def _():
                home(g, k, 0, frm[0]).start()

            order.append((g, k))
    for k in reversed(range(nb)):
        relay(1, k)
    for x in sends[1]:
        x.wait_send()
    for g, k in order:
        for t in range(2):
            home(g, k, t, frm[t]).wait()

        @pl.when(edge)
        def _():
            onward(g, k).wait_send()


def exchange_call(s, chi, clo, phi, plo, layers):
    n = chi.shape[0]
    nb = n // W
    an = pl.BlockSpec(memory_space=pl.ANY)
    vm = pl.BlockSpec(memory_space=pltpu.VMEM)
    D = pltpu.SemaphoreType.DMA
    V = pltpu.VMEM
    return pl.pallas_call(
        functools.partial(exchange_kernel, layers),
        out_shape=jax.ShapeDtypeStruct((2, n, W), bf),
        in_specs=[vm] + [an] * 4, out_specs=an,
        scratch_shapes=[V((n, n), bf), V((n, n), bf), V((nb, W, W), bf), V((nb, W, W), bf), V((nb, 2, W, W), bf),
                        V((2, W, n), bf), V((2, W, n), bf), V((2, nb, 2, W, W // 2), bf), V((2, nb, W, W // 2), bf),
                        D((2, 8, 2)), D((2, 8, 2)), D((2, nb, 2)), D((2, nb, 2)), D((2, nb)), D((2, nb)), D((nb, 2)), D((2,))],
        compiler_params=pltpu.CompilerParams(vmem_limit_bytes=56 * 2**20, collective_id=1, has_side_effects=True),
        cost_estimate=pl.CostEstimate(flops=13 * 10**9, bytes_accessed=3 * 10**7, transcendentals=0),
        name="exchange_solve",
    )(s, chi, clo, phi, plo)


def per_device(features, previous, gradient):
    layers = lax.axis_size("factor") // 8
    shards = lax.axis_size("dp")
    block_size = previous.shape[1]
    weight = (1.0 - decay_rate) / (features.shape[0] * shards)
    blocks, shift = gather_call(features[:, 0, :].T, previous, layers, weight)
    tile_rows = gradient.shape[2]
    flat = gradient[0].reshape(2 * tile_rows, block_size)
    chi, clo, phi, plo, section_one, own_rows = factor_call(blocks, flat, shift)
    result = exchange_call(section_one, chi, clo, phi, plo, layers)
    return (own_rows[None], result[None])


def solution(mesh):
    placed = (P("dp", "factor", None), P("factor", None, None), P("factor", None, "dp", None))
    return jax.shard_map(
        per_device,
        mesh=mesh,
        in_specs=placed,
        out_specs=(P("factor", "dp", None), P("factor", None, None, "dp")),
        check_vma=False,
    )
```
